128 devices in a mesh: lsec: 8 (over y, core), rsec: 4 (over z), mpo: 4 (over x).
Axes of the slice: x: 4, y: 4, z: 4, core: 2. Of those that a mesh axis runs over, the one named last changes fastest.
Arguments:
- wavefunction: bfloat16 [512, 256, 256], P(('lsec', 'rsec')), may hold values from -6 to 6
- left_env: bfloat16 [40, 32, 256, 256], P('mpo', 'lsec'), may hold values from -0.125 to 0.125
- right_env: bfloat16 [40, 16, 256, 256], P('mpo', 'rsec'), may hold values from -0.375 to 0.375
- block_left: int32 [512], P(('lsec', 'rsec')), may hold values from 0 to 31, as said below
- block_right: int32 [512], P(('lsec', 'rsec')), may hold values from 0 to 15, as said below
- channel_class: int32 [40], replicated, may hold values from 0 to 4
- hop_target: int32 [512, 4], replicated, may hold values from 0 to 511, as said below
Outputs:
- result: float32 [512, 256, 256], P(('lsec', 'rsec'), 'mpo')
The draws below stay inside these ranges and needn't reach their ends.
Inputs may be any that keep to these rules, and one draw needn't show every extreme that they name: `block_left`: block k's left sector is one of the 4 sectors [s * 4, (s + 1) * 4) with s = k // 64. `block_right`: block k's right sector is one of the 4 sectors [s * 4, (s + 1) * 4) with s = (k // 16) % 4. `hop_target`: owner pair of a block t is t // 16. Over the 64 entries of the rows of one aligned run of 16 blocks, at most 4 name blocks of any one owner pair; some owner pair is named exactly 4 times by every run.
All inputs are finite; a program needn't handle non-finite values.
Results may differ from the reference program's by a relative error of at most 0.014.
Values may be sent and summed in bfloat16 or wider, within the bound.
No kernel may reach another device: no remote copies, remote signals or barrier semaphores. Data moves between devices by JAX's collectives and lax.ppermute only.
A program may use at most 128 MiB of HBM per device.

```python
import jax
import jax.numpy as jnp
from jax import lax

B = 256
W = 40
NCLS = 5
NHOP = 4
BLK_DEV = 16
SL_DEV = 4
SR_DEV = 4
RGROUPS = 4
OWNERS = 32
NB = 512
NL = 32
NR = 16
GROUPS = 4
GROUP_W = 10
CAP = 4


def draw_block_left(key, part):
    key = jax.random.fold_in(key, 11)
    owner_row = jnp.arange(NB, dtype=jnp.int32) // (BLK_DEV * RGROUPS)
    return owner_row * SL_DEV + jax.random.randint(key, (NB,), 0, SL_DEV, dtype=jnp.int32)


def draw_block_right(key, part):
    key = jax.random.fold_in(key, 23)
    owner_col = jnp.arange(NB, dtype=jnp.int32) // BLK_DEV % RGROUPS
    return owner_col * SR_DEV + jax.random.randint(key, (NB,), 0, SR_DEV, dtype=jnp.int32)


def draw_hop_target(key, part):
    key = jax.random.fold_in(key, 37)
    key_full, key_score, key_shuffle, key_inner = jax.random.split(key, 4)
    slot_total = OWNERS * CAP
    item_count = BLK_DEV * NHOP
    forced = jax.random.randint(key_full, (), 0, OWNERS, dtype=jnp.int32)
    slot_range = jnp.arange(slot_total, dtype=jnp.int32)
    scores = jax.random.randint(key_score, (OWNERS, slot_total), 0, 2 ** 20, dtype=jnp.int32)
    scores = scores * slot_total + slot_range[None, :]
    scores = jnp.where((slot_range // CAP)[None, :] == forced, -1 - slot_range[None, :], scores)
    chosen = jnp.argsort(scores, axis=1, stable=True)[:, :item_count]
    shuffle = jax.random.randint(key_shuffle, (OWNERS, item_count), 0, 2 ** 20, dtype=jnp.int32)
    shuffle = shuffle * item_count + jnp.arange(item_count, dtype=jnp.int32)[None, :]
    order = jnp.argsort(shuffle, axis=1, stable=True)
    chosen = jnp.take_along_axis(chosen, order, axis=1)
    owner_pick = (chosen // CAP).astype(jnp.int32)
    inner_pick = jax.random.randint(key_inner, (OWNERS, item_count), 0, BLK_DEV, dtype=jnp.int32)
    targets = owner_pick * BLK_DEV + inner_pick
    return targets.reshape(NB, NHOP)


def touch_ends(values, key, least, top_value):
    index_at = [jax.random.randint(jax.random.fold_in(key, axis), (), 0, length) for axis, length in enumerate(values.shape)]
    longest = values.shape.index(max(values.shape))
    next_to = index_at[:longest] + [(index_at[longest] + 1) % values.shape[longest]] + index_at[longest + 1:]
    return values.at[tuple(index_at)].set(least).at[tuple(next_to)].set(top_value)


def level_of(key, extent, pieces, least, top_value):
    gain, own = 1.0, jax.random.fold_in(key, 6)
    for dim, parts in pieces:
        draws = jnp.exp(jax.random.uniform(jax.random.fold_in(own, dim), (parts,), jnp.float32, least / len(pieces), top_value / len(pieces)))
        gain = gain * jnp.repeat(draws, extent[dim] // parts).reshape([-1 if axis == dim else 1 for axis in range(len(extent))])
    return gain


def normal_values(own_key, dims, deviation, limit, cuts=(), kind=jnp.bfloat16):
    values = jax.random.normal(own_key, dims, jnp.float32) * deviation
    if len(cuts) > 0:
        values = level_of(own_key, dims, cuts, -0.22, 0.18) * values
    return jnp.clip(values, min=-limit, max=limit).astype(kind)


def setup_inputs(seed: int = 0) -> dict:
    seeds = jax.random.split(jax.random.key(seed), 8)
    return {
        "wavefunction": normal_values(seeds[0], (NB, B, B), 1.0, 6.0, ((0, 32),)),
        "left_env": normal_values(seeds[1], (W, NL, B, B), (8 * B) ** -0.5, 0.125, ((0, 4), (1, 8))),
        "right_env": normal_values(seeds[2], (W, NR, B, B), B ** -0.5, 0.375, ((0, 4), (1, 4))),
        "block_left": draw_block_left(jax.random.fold_in(seeds[7], 71), 0),
        "block_right": draw_block_right(jax.random.fold_in(seeds[7], 71), 0),
        "channel_class": touch_ends(jax.random.randint(seeds[5], (W,), 0, NCLS), jax.random.fold_in(seeds[5], 1), 0, NCLS - 1).astype(jnp.int32),
        "hop_target": draw_hop_target(jax.random.fold_in(seeds[7], 71), 0),
    }


def group_terms(psi_blocks, left_ids, right_ids, left_env, right_env, channel_class, group_index):
    start = group_index * GROUP_W

    def channel_step(totals, offset):
        channel = start + offset
        left_pick = jnp.take(lax.dynamic_index_in_dim(left_env, channel, 0, False), left_ids, axis=0)
        right_pick = jnp.take(lax.dynamic_index_in_dim(right_env, channel, 0, False), right_ids, axis=0)
        half_product = jnp.einsum("kab,kbc->kac", left_pick.astype(jnp.float32), psi_blocks.astype(jnp.float32)).astype(jnp.bfloat16)
        half_product = lax.optimization_barrier(half_product)
        full_product = jnp.einsum("kac,kcd->kad", half_product.astype(jnp.float32), right_pick.astype(jnp.float32))
        class_id = lax.dynamic_index_in_dim(channel_class, channel, 0, False)
        class_mask = (jnp.arange(NCLS, dtype=jnp.int32) == class_id).astype(jnp.float32)
        return totals + class_mask[:, None, None, None] * full_product[None], None

    totals = jnp.zeros((NCLS,) + psi_blocks.shape, jnp.float32)
    totals, _ = lax.scan(channel_step, totals, jnp.arange(GROUP_W, dtype=jnp.int32))
    rounded = lax.optimization_barrier(totals.astype(jnp.bfloat16))
    return rounded.astype(jnp.float32)


def reference(wavefunction, left_env, right_env, block_left, block_right, channel_class, hop_target):
    owner_total = NB // BLK_DEV

    def owner_step(result, owner_index):
        first_row = owner_index * BLK_DEV
        psi_blocks = lax.dynamic_slice_in_dim(wavefunction, first_row, BLK_DEV, 0)
        left_ids = lax.dynamic_slice_in_dim(block_left, first_row, BLK_DEV, 0)
        right_ids = lax.dynamic_slice_in_dim(block_right, first_row, BLK_DEV, 0)
        targets = lax.dynamic_slice_in_dim(hop_target, first_row, BLK_DEV, 0)
        for group_index in range(GROUPS):
            terms = group_terms(psi_blocks, left_ids, right_ids, left_env, right_env, channel_class, group_index)
            own_part = lax.dynamic_slice_in_dim(result, first_row, BLK_DEV, 0) + terms[0]
            result = lax.dynamic_update_slice_in_dim(result, own_part, first_row, 0)
            moved = jnp.transpose(terms[1:], (1, 0, 2, 3)).reshape(BLK_DEV * NHOP, B, B)
            result = result.at[targets.reshape(-1)].add(moved)
        return result, None

    result = jnp.zeros((NB, B, B), jnp.float32)
    result, _ = lax.scan(owner_step, result, jnp.arange(owner_total, dtype=jnp.int32))
    return result
```

```python
import functools

import jax
import jax.numpy as jnp
from jax import lax
from jax.experimental import pallas as pl
from jax.experimental.pallas import tpu as pltpu
from jax.sharding import PartitionSpec as P

LANES = 128
ROW_CHUNKS = (16, 16, 16, 16)


def products_kernel(
    chunks, x_ref, left_ids, right_ids, class_ids, first_ref, psi_ref, left_hbm, right_hbm, *rest
):
    chunk_count = len(chunks)
    outs = rest[: 4 * chunk_count]
    left_ref, right_ref, half_ref, acc_ref, left_sems, right_sems = rest[4 * chunk_count :]
    channels = left_ref.shape[0]
    classes = acc_ref.shape[0]
    block = acc_ref.shape[1]
    quarter = block // 4
    step = pl.program_id(0)

    def left_copy(w):
        return pltpu.make_async_copy(left_hbm.at[w], left_ref.at[w], left_sems.at[w])

    def right_copy(w):
        return pltpu.make_async_copy(right_hbm.at[w], right_ref.at[w], right_sems.at[w])

    @pl.when(step == 0)
    def _():
        for w in range(channels):
            left_copy(w).start()
        for w in range(channels):
            right_copy(w).start()
        acc_ref[...] = jnp.zeros_like(acc_ref)
        for w in range(channels):
            left_copy(w).wait()
        for w in range(channels):
            right_copy(w).wait()

    left_id = left_ids[step]
    right_id = right_ids[step]
    psi = psi_ref[0]
    for w in range(channels):
        half_ref[w] = jnp.dot(
            left_ref[w, left_id], psi, preferred_element_type=jnp.float32
        ).astype(jnp.bfloat16)
    for w in range(channels):
        full = jnp.dot(half_ref[w], right_ref[w, right_id], preferred_element_type=jnp.float32)
        member = class_ids[w]
        before = acc_ref[member]
        acc_ref[member] = jnp.where(first_ref[w] != 0, 0.0, before) + full

    x = x_ref[0]
    mirror = 3 - x
    beside = x ^ 1
    across = mirror ^ 1
    orders = ((x, mirror, beside, across), (x, beside, mirror, across))
    start = 0
    for j, rows in enumerate(chunks):
        for s in range(2):
            keep, send = outs[4 * j + 2 * s], outs[4 * j + 2 * s + 1]
            for place, q in enumerate(orders[s]):
                target = keep if place < 2 else send
                at = pl.multiple_of(q * quarter + start, 16)
                for c in range(classes):
                    target[c, place % 2] = acc_ref[
                        c, pl.ds(at, rows), s * LANES : (s + 1) * LANES
                    ].astype(jnp.bfloat16)
        start += rows


def products(x, left_ids, right_ids, class_ids, first, psi, left_env, right_env, classes, chunks):
    blocks, block, _ = psi.shape
    channels = left_env.shape[0]
    out_shape, out_specs = [], []
    for rows in chunks:
        for _ in range(4):
            out_shape.append(
                jax.ShapeDtypeStruct((blocks * classes, 2, rows, LANES), jnp.bfloat16)
            )
            out_specs.append(
                pl.BlockSpec((classes, 2, rows, LANES), lambda k, *_: (k, 0, 0, 0))
            )
    return pl.pallas_call(
        functools.partial(products_kernel, chunks),
        out_shape=out_shape,
        grid_spec=pltpu.PrefetchScalarGridSpec(
            num_scalar_prefetch=5,
            grid=(blocks,),
            in_specs=[
                pl.BlockSpec((1, block, block), lambda k, *_: (k, 0, 0)),
                pl.BlockSpec(memory_space=pl.ANY),
                pl.BlockSpec(memory_space=pl.ANY),
            ],
            out_specs=out_specs,
            scratch_shapes=[
                pltpu.VMEM(left_env.shape, jnp.bfloat16),
                pltpu.VMEM(right_env.shape, jnp.bfloat16),
                pltpu.VMEM((channels, block, block), jnp.bfloat16),
                pltpu.VMEM((classes, block, block), jnp.float32),
                pltpu.SemaphoreType.DMA((channels,)),
                pltpu.SemaphoreType.DMA((channels,)),
            ],
        ),
        compiler_params=pltpu.CompilerParams(vmem_limit_bytes=40 * 2**20),
        cost_estimate=pl.CostEstimate(
            flops=4 * channels * blocks * block**3,
            bytes_accessed=2 * (left_env.size + right_env.size + psi.size * (1 + classes)),
            transcendentals=0,
        ),
        name="products",
    )(x, left_ids, right_ids, class_ids, first, psi, left_env, right_env)


def slots_kernel(classes, items, keep_a, got_a, last_a, keep_b, got_b, last_b, slots, own):
    slot_count = slots.shape[0]
    block_count = own.shape[0]

    def total(keep, got, last, i):
        return (
            keep[i, 0].astype(jnp.float32)
            + got[i, 0].astype(jnp.float32)
            + last[i].astype(jnp.float32)
        )

    def fill(p, _):
        i = items[p]
        slots[p, :, :LANES] = total(keep_a, got_a, last_a, i).astype(jnp.bfloat16)
        slots[p, :, LANES:] = total(keep_b, got_b, last_b, i).astype(jnp.bfloat16)
        return 0

    lax.fori_loop(0, slot_count, fill, 0, unroll=4)

    def stay(k, _):
        i = k * classes
        own[k, :, :LANES] = total(keep_a, got_a, last_a, i)
        own[k, :, LANES:] = total(keep_b, got_b, last_b, i)
        return 0

    lax.fori_loop(0, block_count, stay, 0, unroll=4)


def fill_slots(items, parts, classes):
    keep_a, got_a, last_a, keep_b, got_b, last_b = parts
    count, _, rows, _ = keep_a.shape
    blocks = count // classes
    pair = pl.BlockSpec((count, 1, rows, LANES), lambda i, *_: (0, 0, 0, 0))
    one = pl.BlockSpec((count, rows, LANES), lambda i, *_: (0, 0, 0))
    slot_count = items.shape[0]
    return pl.pallas_call(
        functools.partial(slots_kernel, classes),
        out_shape=(
            jax.ShapeDtypeStruct((slot_count, rows, 2 * LANES), jnp.bfloat16),
            jax.ShapeDtypeStruct((blocks, rows, 2 * LANES), jnp.float32),
        ),
        grid_spec=pltpu.PrefetchScalarGridSpec(
            num_scalar_prefetch=1,
            grid=(1,),
            in_specs=[pair, pair, one, pair, pair, one],
            out_specs=(
                pl.BlockSpec((slot_count, rows, 2 * LANES), lambda i, *_: (0, 0, 0)),
                pl.BlockSpec((blocks, rows, 2 * LANES), lambda i, *_: (0, 0, 0)),
            ),
        ),
        compiler_params=pltpu.CompilerParams(vmem_limit_bytes=32 * 2**20),
        name="fill_slots",
    )(items, keep_a, got_a, last_a, keep_b, got_b, last_b)


def gather_kernel(places, received, own, *rest):
    result = rest[-1]
    result[...] = own[...]

    def add(p, _):
        b = places[p]

        @pl.when(b >= 0)
        def _():
            result[b] += received[p].astype(jnp.float32)

        return 0

    lax.fori_loop(0, received.shape[0], add, 0)


def add_received(places, received, own, so_far, start, quarter):
    blocks, rows, width = own.shape
    at = start // rows
    operands = [places, received, own]
    in_specs = [
        pl.BlockSpec(received.shape, lambda i, *_: (0, 0, 0)),
        pl.BlockSpec(own.shape, lambda i, *_: (0, 0, 0)),
    ]
    aliases = {}
    if so_far is not None:
        operands.append(so_far)
        in_specs.append(pl.BlockSpec(memory_space=pl.ANY))
        aliases = {3: 0}
    return pl.pallas_call(
        gather_kernel,
        out_shape=jax.ShapeDtypeStruct((blocks, quarter, width), jnp.float32),
        grid_spec=pltpu.PrefetchScalarGridSpec(
            num_scalar_prefetch=1,
            grid=(1,),
            in_specs=in_specs,
            out_specs=pl.BlockSpec((blocks, rows, width), lambda i, *_: (0, at, 0)),
        ),
        input_output_aliases=aliases,
        compiler_params=pltpu.CompilerParams(vmem_limit_bytes=32 * 2**20),
        name="add_received",
    )(*operands)


def item_places(targets, block_count):
    destined = targets // block_count
    count = targets.shape[-1]
    earlier = jnp.arange(count)[:, None] > jnp.arange(count)[None, :]
    same = (destined[..., :, None] == destined[..., None, :]) & earlier
    return destined, jnp.sum(same.astype(jnp.int32), axis=-1)


def shards(wavefunction, left_env, right_env, block_left, block_right, channel_class, hop_target):
    block_count, block_size, _ = wavefunction.shape
    group_width = left_env.shape[0]
    hop_count = hop_target.shape[1]
    classes = hop_count + 1
    owners = lax.axis_size("lsec") * lax.axis_size("rsec")
    item_count = block_count * hop_count
    capacity = 2 * ((item_count + owners - 1) // owners)
    slot_count = owners * capacity
    quarter = block_size // lax.axis_size("mpo")
    me = lax.axis_index("lsec") * lax.axis_size("rsec") + lax.axis_index("rsec")
    x = lax.axis_index("mpo")
    local_left = block_left - lax.axis_index("lsec") * left_env.shape[1]
    local_right = block_right - lax.axis_index("rsec") * right_env.shape[1]
    group_class = lax.dynamic_slice_in_dim(channel_class, x * group_width, group_width, 0)
    w = jnp.arange(group_width)
    seen = jnp.any((group_class[:, None] == group_class[None, :]) & (w[:, None] > w[None, :]), 1)
    first = jnp.logical_not(seen).astype(jnp.int32)

    parts = products(
        x.astype(jnp.int32)[None],
        local_left,
        local_right,
        group_class,
        first,
        wavefunction,
        left_env,
        right_env,
        classes,
        ROW_CHUNKS,
    )

    targets = hop_target.reshape(owners, item_count)
    own_targets = lax.dynamic_index_in_dim(targets, me, 0, False)
    destined, slot = item_places(own_targets, block_count)
    position = destined * capacity + slot
    held = position[:, None] == jnp.arange(slot_count, dtype=jnp.int32)[None, :]
    index = jnp.arange(item_count, dtype=jnp.int32)
    index = (index // hop_count) * classes + 1 + index % hop_count
    slot_items = jnp.sum(jnp.where(held, index[:, None], 0), axis=0)
    destined_all, slot_all = item_places(targets, block_count)
    mine = (destined_all == me)[:, :, None] & (
        slot_all[:, :, None] == jnp.arange(capacity, dtype=jnp.int32)
    )
    local = targets - me * block_count + 1
    places = jnp.sum(jnp.where(mine, local[:, :, None], 0), axis=1).reshape(slot_count) - 1

    beside = [(i, i ^ 1) for i in range(4)]
    mirror = [(i, 3 - i) for i in range(4)]
    result = None
    start = 0
    for j, rows in enumerate(ROW_CHUNKS):
        keep_a, send_a, keep_b, send_b = parts[4 * j : 4 * j + 4]
        got_a = lax.ppermute(send_a, "mpo", beside)
        got_b = lax.ppermute(send_b, "mpo", mirror)

        def second(keep, got):
            return (
                keep[:, 1].astype(jnp.float32) + got[:, 1].astype(jnp.float32)
            ).astype(jnp.bfloat16)

        last_a = lax.ppermute(second(keep_a, got_a), "mpo", mirror)
        last_b = lax.ppermute(second(keep_b, got_b), "mpo", beside)
        slots, own = fill_slots(
            slot_items, (keep_a, got_a, last_a, keep_b, got_b, last_b), classes
        )
        received = lax.all_to_all(slots, ("lsec", "rsec"), 0, 0, tiled=True)
        result = add_received(places, received, own, result, start, quarter)
        start += rows
    return result


def solution(mesh):
    in_specs = (
        P(("lsec", "rsec"), None, None),
        P("mpo", "lsec", None, None),
        P("mpo", "rsec", None, None),
        P(("lsec", "rsec")),
        P(("lsec", "rsec")),
        P(),
        P(),
    )
    out_specs = P(("lsec", "rsec"), "mpo", None)
    return jax.shard_map(shards, mesh=mesh, in_specs=in_specs, out_specs=out_specs, check_vma=False)
```

```python
import functools

import jax
import jax.numpy as jnp
from jax import lax
from jax.experimental import pallas as pl
from jax.experimental.pallas import tpu as pltpu
from jax.sharding import PartitionSpec as P

LANES = 128
EARLY_ROWS = 16
ROW_CHUNKS = (16, 32)


def products_kernel(
    chunks, x_ref, left_ids, right_ids, class_ids, first_ref, psi_ref, left_hbm, right_hbm, *rest
):
    count = 2 + 4 * len(chunks)
    early_own, early_moved, *outs = rest[:count]
    left_ref, right_ref, half_ref, acc_ref, left_sems, right_sems = rest[count:]
    channels = left_ref.shape[0]
    classes = acc_ref.shape[0]
    quarter = acc_ref.shape[1] // 4
    step = pl.program_id(0)

    def left_copy(w):
        return pltpu.make_async_copy(left_hbm.at[w], left_ref.at[w], left_sems.at[w])

    def right_copy(w):
        return pltpu.make_async_copy(right_hbm.at[w], right_ref.at[w], right_sems.at[w])

    def multiply(arriving):
        left_id = left_ids[step]
        right_id = right_ids[step]
        for w in range(channels):
            if arriving:
                left_copy(w).wait()
            half_ref[w] = jnp.dot(
                left_ref[w, left_id], psi_ref[0], preferred_element_type=jnp.float32
            ).astype(jnp.bfloat16)
        for w in range(channels):
            if arriving:
                right_copy(w).wait()
            full = jnp.dot(half_ref[w], right_ref[w, right_id], preferred_element_type=jnp.float32)
            member = class_ids[w]
            before = acc_ref[member]
            acc_ref[member] = jnp.where(first_ref[w] != 0, 0.0, before) + full

    @pl.when(step == 0)
    def _():
        for w in range(channels):
            left_copy(w).start()
        for w in range(channels):
            right_copy(w).start()
        acc_ref[...] = jnp.zeros_like(acc_ref)
        multiply(True)

    @pl.when(step != 0)
    def _():
        multiply(False)

    x = x_ref[0]
    mirror = 3 - x
    beside = x ^ 1
    across = mirror ^ 1
    orders = ((x, mirror, beside, across), (x, beside, mirror, across))
    for q in range(4):
        rows = slice(q * EARLY_ROWS, (q + 1) * EARLY_ROWS)
        at = q * quarter
        early_own[0, rows] = acc_ref[0, at : at + EARLY_ROWS].astype(jnp.bfloat16)
        for c in range(1, classes):
            early_moved[c - 1, rows] = acc_ref[c, at : at + EARLY_ROWS].astype(jnp.bfloat16)
    start = EARLY_ROWS
    for j, rows in enumerate(chunks):
        for s in range(2):
            keep, send = outs[4 * j + 2 * s], outs[4 * j + 2 * s + 1]
            for place, q in enumerate(orders[s]):
                target = keep if place < 2 else send
                at = pl.multiple_of(q * quarter + start, 16)
                for c in range(classes):
                    target[place % 2, c] = acc_ref[
                        c, pl.ds(at, rows), s * LANES : (s + 1) * LANES
                    ].astype(jnp.bfloat16)
        start += rows


def products(x, left_ids, right_ids, class_ids, first, psi, left_env, right_env, classes, chunks):
    blocks, block, _ = psi.shape
    channels = left_env.shape[0]
    early = 4 * EARLY_ROWS
    hops = classes - 1
    out_shape = [
        pltpu.HBM((blocks, early, block), jnp.bfloat16),
        pltpu.HBM((blocks * hops, early, block), jnp.bfloat16),
    ]
    out_specs = [
        pl.BlockSpec((1, early, block), lambda k, *_: (k, 0, 0)),
        pl.BlockSpec((hops, early, block), lambda k, *_: (k, 0, 0)),
    ]
    for rows in chunks:
        for _ in range(4):
            out_shape.append(pltpu.HBM((2, blocks * classes, rows, LANES), jnp.bfloat16))
            out_specs.append(pl.BlockSpec((2, classes, rows, LANES), lambda k, *_: (0, k, 0, 0)))
    return pl.pallas_call(
        functools.partial(products_kernel, chunks),
        out_shape=out_shape,
        grid_spec=pltpu.PrefetchScalarGridSpec(
            num_scalar_prefetch=5,
            grid=(blocks,),
            in_specs=[
                pl.BlockSpec((1, block, block), lambda k, *_: (k, 0, 0)),
                pl.BlockSpec(memory_space=pl.ANY),
                pl.BlockSpec(memory_space=pl.ANY),
            ],
            out_specs=out_specs,
            scratch_shapes=[
                pltpu.VMEM(left_env.shape, jnp.bfloat16),
                pltpu.VMEM(right_env.shape, jnp.bfloat16),
                pltpu.VMEM((channels, block, block), jnp.bfloat16),
                pltpu.VMEM((classes, block, block), jnp.float32),
                pltpu.SemaphoreType.DMA((channels,)),
                pltpu.SemaphoreType.DMA((channels,)),
            ],
        ),
        compiler_params=pltpu.CompilerParams(vmem_limit_bytes=40 * 2**20),
        cost_estimate=pl.CostEstimate(
            flops=4 * channels * blocks * block**3,
            bytes_accessed=2 * (left_env.size + right_env.size + psi.size * (1 + classes)),
            transcendentals=0,
        ),
        name="products",
    )(x, left_ids, right_ids, class_ids, first, psi, left_env, right_env)


def place_kernel(items, moved, slots):
    def fill(p, _):
        slots[p] = moved[items[p]]
        return 0

    lax.fori_loop(0, slots.shape[0], fill, 0, unroll=4)


def place_items(items, moved):
    slot_count = items.shape[0]
    _, rows, width = moved.shape
    return pl.pallas_call(
        place_kernel,
        out_shape=pltpu.HBM((slot_count, rows, width), jnp.bfloat16),
        grid_spec=pltpu.PrefetchScalarGridSpec(
            num_scalar_prefetch=1,
            grid=(1,),
            in_specs=[pl.BlockSpec(moved.shape, lambda i, *_: (0, 0, 0))],
            out_specs=pl.BlockSpec((slot_count, rows, width), lambda i, *_: (0, 0, 0)),
        ),
        compiler_params=pltpu.CompilerParams(vmem_limit_bytes=32 * 2**20),
        name="place_items",
    )(items, moved)


def merge_kernel(places, received, own, out, acc):
    blocks, rows, _ = own.shape
    acc[:blocks] = own[...].astype(jnp.float32)

    def add(p, _):
        acc[places[p]] += received[p].astype(jnp.float32)
        return 0

    lax.fori_loop(0, received.shape[0], add, 0, unroll=4)
    for q in range(4):
        out[q] = acc[:blocks, q * (rows // 4) : (q + 1) * (rows // 4)].astype(jnp.bfloat16)


def merge_early(places, received, own):
    blocks, rows, width = own.shape
    return pl.pallas_call(
        merge_kernel,
        out_shape=pltpu.HBM((4, blocks, rows // 4, width), jnp.bfloat16),
        grid_spec=pltpu.PrefetchScalarGridSpec(
            num_scalar_prefetch=1,
            grid=(1,),
            in_specs=[
                pl.BlockSpec(received.shape, lambda i, *_: (0, 0, 0)),
                pl.BlockSpec(own.shape, lambda i, *_: (0, 0, 0)),
            ],
            out_specs=pl.BlockSpec((4, blocks, rows // 4, width), lambda i, *_: (0, 0, 0, 0)),
            scratch_shapes=[pltpu.VMEM((blocks + 1, rows, width), jnp.float32)],
        ),
        compiler_params=pltpu.CompilerParams(vmem_limit_bytes=32 * 2**20),
        name="merge_early",
    )(places, received, own)


def slots_kernel(classes, items, keep_a, got_a, last_a, keep_b, got_b, last_b, slots, own):
    slot_count = slots.shape[0]
    block_count = own.shape[0]

    def total(keep, got, last, i):
        return (
            keep[0, i].astype(jnp.float32)
            + got[0, i].astype(jnp.float32)
            + last[i].astype(jnp.float32)
        )

    def fill(p, _):
        i = items[p]
        slots[p, :, :LANES] = total(keep_a, got_a, last_a, i).astype(jnp.bfloat16)
        slots[p, :, LANES:] = total(keep_b, got_b, last_b, i).astype(jnp.bfloat16)
        return 0

    lax.fori_loop(0, slot_count, fill, 0, unroll=4)

    def stay(k, _):
        i = k * classes
        own[k, :, :LANES] = total(keep_a, got_a, last_a, i)
        own[k, :, LANES:] = total(keep_b, got_b, last_b, i)
        return 0

    lax.fori_loop(0, block_count, stay, 0, unroll=4)


def fill_slots(items, parts, classes):
    keep_a, got_a, last_a, keep_b, got_b, last_b = parts
    _, count, rows, _ = keep_a.shape
    blocks = count // classes
    pair = pl.BlockSpec((1, count, rows, LANES), lambda i, *_: (0, 0, 0, 0))
    one = pl.BlockSpec((count, rows, LANES), lambda i, *_: (0, 0, 0))
    slot_count = items.shape[0]
    return pl.pallas_call(
        functools.partial(slots_kernel, classes),
        out_shape=(
            pltpu.HBM((slot_count, rows, 2 * LANES), jnp.bfloat16),
            pltpu.HBM((blocks, rows, 2 * LANES), jnp.float32),
        ),
        grid_spec=pltpu.PrefetchScalarGridSpec(
            num_scalar_prefetch=1,
            grid=(1,),
            in_specs=[pair, pair, one, pair, pair, one],
            out_specs=(
                pl.BlockSpec((slot_count, rows, 2 * LANES), lambda i, *_: (0, 0, 0)),
                pl.BlockSpec((blocks, rows, 2 * LANES), lambda i, *_: (0, 0, 0)),
            ),
        ),
        compiler_params=pltpu.CompilerParams(vmem_limit_bytes=32 * 2**20),
        name="fill_slots",
    )(items, keep_a, got_a, last_a, keep_b, got_b, last_b)


def add_received(places, received, own, so_far, start):
    blocks, rows, width = own.shape

    def kernel(places, received, own, so_far, result, acc, sem):
        acc[:blocks] = own[...]

        def add(p, _):
            acc[places[p]] += received[p].astype(jnp.float32)
            return 0

        lax.fori_loop(0, received.shape[0], add, 0, unroll=4)
        copy = pltpu.make_async_copy(
            acc.at[pl.ds(0, blocks)], result.at[:, pl.ds(start, rows)], sem
        )
        copy.start()
        copy.wait()

    return pl.pallas_call(
        kernel,
        out_shape=pltpu.HBM(so_far.shape, jnp.float32),
        grid_spec=pltpu.PrefetchScalarGridSpec(
            num_scalar_prefetch=1,
            grid=(1,),
            in_specs=[
                pl.BlockSpec(received.shape, lambda i, *_: (0, 0, 0)),
                pl.BlockSpec(own.shape, lambda i, *_: (0, 0, 0)),
                pl.BlockSpec(memory_space=pl.ANY),
            ],
            out_specs=pl.BlockSpec(memory_space=pl.ANY),
            scratch_shapes=[
                pltpu.VMEM((blocks + 1, rows, width), jnp.float32),
                pltpu.SemaphoreType.DMA,
            ],
        ),
        input_output_aliases={3: 0},
        compiler_params=pltpu.CompilerParams(vmem_limit_bytes=32 * 2**20),
        name="add_received",
    )(places, received, own, so_far)


def place_early(scattered, quarter):
    blocks, rows, width = scattered.shape

    def kernel(scattered, result):
        result[...] = scattered[...].astype(jnp.float32)

    return pl.pallas_call(
        kernel,
        out_shape=pltpu.HBM((blocks, quarter, width), jnp.float32),
        grid=(1,),
        in_specs=[pl.BlockSpec((blocks, rows, width), lambda i: (0, 0, 0))],
        out_specs=pl.BlockSpec((blocks, rows, width), lambda i: (0, 0, 0)),
        name="place_early",
    )(scattered)


def item_places(targets, block_count):
    destined = targets // block_count
    count = targets.shape[-1]
    earlier = jnp.arange(count)[:, None] > jnp.arange(count)[None, :]
    same = (destined[..., :, None] == destined[..., None, :]) & earlier
    return destined, jnp.sum(same.astype(jnp.int32), axis=-1)


def shards(wavefunction, left_env, right_env, block_left, block_right, channel_class, hop_target):
    block_count, block_size, _ = wavefunction.shape
    group_width = left_env.shape[0]
    hop_count = hop_target.shape[1]
    classes = hop_count + 1
    owners = lax.axis_size("lsec") * lax.axis_size("rsec")
    item_count = block_count * hop_count
    capacity = 2 * ((item_count + owners - 1) // owners)
    slot_count = owners * capacity
    quarter = block_size // lax.axis_size("mpo")
    me = lax.axis_index("lsec") * lax.axis_size("rsec") + lax.axis_index("rsec")
    x = lax.axis_index("mpo")
    local_left = block_left - lax.axis_index("lsec") * left_env.shape[1]
    local_right = block_right - lax.axis_index("rsec") * right_env.shape[1]
    group_class = lax.dynamic_slice_in_dim(channel_class, x * group_width, group_width, 0)
    w = jnp.arange(group_width)
    seen = jnp.any((group_class[:, None] == group_class[None, :]) & (w[:, None] > w[None, :]), 1)
    first = jnp.logical_not(seen).astype(jnp.int32)

    early_own, early_moved, *parts = products(
        x.astype(jnp.int32)[None],
        local_left,
        local_right,
        group_class,
        first,
        wavefunction,
        left_env,
        right_env,
        classes,
        ROW_CHUNKS,
    )

    targets = hop_target.reshape(owners, item_count)
    own_targets = lax.dynamic_index_in_dim(targets, me, 0, False)
    destined, slot = item_places(own_targets, block_count)
    position = destined * capacity + slot
    held = position[:, None] == jnp.arange(slot_count, dtype=jnp.int32)[None, :]
    index = jnp.arange(item_count, dtype=jnp.int32)
    index = (index // hop_count) * classes + 1 + index % hop_count
    slot_items = jnp.sum(jnp.where(held, index[:, None], 0), axis=0)
    destined_all, slot_all = item_places(targets, block_count)
    mine = (destined_all == me)[:, :, None] & (
        slot_all[:, :, None] == jnp.arange(capacity, dtype=jnp.int32)
    )
    local = targets - (me + 1) * block_count
    places = jnp.sum(jnp.where(mine, local[:, :, None], 0), axis=1).reshape(slot_count)
    places = places + block_count
    plain_items = jnp.sum(
        jnp.where(held, jnp.arange(item_count, dtype=jnp.int32)[:, None], 0), axis=0
    )

    early = lax.all_to_all(
        place_items(plain_items, early_moved), ("lsec", "rsec"), 0, 0, tiled=True
    )
    merged = merge_early(places, early, early_own)
    scattered = lax.psum_scatter(merged, "mpo", scatter_dimension=0, tiled=False)
    result = place_early(scattered, quarter)

    beside = [(i, i ^ 1) for i in range(4)]
    mirror = [(i, 3 - i) for i in range(4)]
    start = EARLY_ROWS
    for j, rows in enumerate(ROW_CHUNKS):
        keep_a, send_a, keep_b, send_b = parts[4 * j : 4 * j + 4]
        got_a = lax.ppermute(send_a, "mpo", beside)
        got_b = lax.ppermute(send_b, "mpo", mirror)

        def second(keep, got):
            return (keep[1].astype(jnp.float32) + got[1].astype(jnp.float32)).astype(jnp.bfloat16)

        last_a = lax.ppermute(second(keep_a, got_a), "mpo", mirror)
        last_b = lax.ppermute(second(keep_b, got_b), "mpo", beside)
        slots, own = fill_slots(
            slot_items, (keep_a, got_a, last_a, keep_b, got_b, last_b), classes
        )
        received = lax.all_to_all(slots, ("lsec", "rsec"), 0, 0, tiled=True)
        result = add_received(places, received, own, result, start)
        start += rows
    return result


def solution(mesh):
    in_specs = (
        P(("lsec", "rsec"), None, None),
        P("mpo", "lsec", None, None),
        P("mpo", "rsec", None, None),
        P(("lsec", "rsec")),
        P(("lsec", "rsec")),
        P(),
        P(),
    )
    out_specs = P(("lsec", "rsec"), "mpo", None)
    return jax.shard_map(shards, mesh=mesh, in_specs=in_specs, out_specs=out_specs, check_vma=False)
```

```python
import functools

import jax
import jax.numpy as jnp
from jax import lax
from jax.experimental import pallas as pl
from jax.experimental.pallas import tpu as pltpu
from jax.sharding import PartitionSpec as P

LANES = 128
EARLY_ROWS = 16
CHUNKS = (16, 32)
BF16 = jnp.bfloat16
F32 = jnp.float32


def small_cost():
    return pl.CostEstimate(flops=1, bytes_accessed=1, transcendentals=0)


def large_cost():
    return pl.CostEstimate(flops=6 * 10**10, bytes_accessed=1, transcendentals=0)


def whole(shape):
    return pl.BlockSpec(shape, lambda i, *_: (0,) * len(shape))


def relative_quarters(x):
    return x, x ^ 1, 3 - x, (3 - x) ^ 1


def products_kernel(
    capacity, device, block_left, block_right, channel_class, own_targets, psi_ref, left_hbm,
    right_hbm, *rest
):
    *outs, left_ref, right_ref, half_ref, acc_ref, stage_ref = rest[:-8]
    seen_ref, first_ref, slot_ref, left_here, right_here, left_sems, right_sems, slot_sems = rest[-8:]
    own, slots_hbm, *chunk_outs = outs
    channels, left_count, _, _ = left_ref.shape
    right_count = right_ref.shape[1]
    classes = acc_ref.shape[0]
    hops = classes - 1
    quarter = acc_ref.shape[1] // 4
    step = pl.program_id(0)
    x = device[0]
    left_id = block_left[step] - device[1] * left_count
    right_id = block_right[step] - device[2] * right_count

    def left_copy(i):
        return pltpu.make_async_copy(left_hbm.at[:, i], left_ref.at[:, i], left_sems.at[i])

    def right_copy(i):
        return pltpu.make_async_copy(right_hbm.at[:, i], right_ref.at[:, i], right_sems.at[i])

    def slot_copy(k, h):
        side = lax.rem(k, 2)
        return pltpu.make_async_copy(
            stage_ref.at[side, h], slots_hbm.at[slot_ref[k * hops + h]], slot_sems.at[side, h]
        )

    def need(copy, here, i):
        @pl.when(here[i] == 0)
        def _():
            copy(i).wait()
            here[i] = 1

    @pl.when(step == 0)
    def _():
        for i in range(left_count):
            left_here[i] = 0
        for i in range(right_count):
            right_here[i] = 0
        for turn in range(max(left_count, right_count)):
            if turn < left_count:
                left_copy(lax.rem(left_id + turn, left_count)).start()
            if turn < right_count:
                right_copy(lax.rem(right_id + turn, right_count)).start()
        acc_ref[...] = jnp.zeros_like(acc_ref)
        blocks = pl.num_programs(0)
        for i in range(seen_ref.shape[0]):
            seen_ref[i] = 0

        def place(i, _):
            owner = lax.div(own_targets[i], blocks)
            earlier = seen_ref[owner]
            slot_ref[i] = owner * capacity + earlier
            seen_ref[owner] = earlier + 1
            return 0

        lax.fori_loop(0, slot_ref.shape[0], place, 0)
        for w in range(channels):
            before = [channel_class[x * channels + v] for v in range(w)]
            same = [jnp.int32(b == channel_class[x * channels + w]) for b in before]
            first_ref[w] = jnp.int32(sum(same, jnp.int32(0)) == 0)

    @pl.when(step >= 2)
    def _():
        for h in range(hops):
            slot_copy(step - 2, h).wait()

    need(left_copy, left_here, left_id)
    need(right_copy, right_here, right_id)

    for w in range(channels):
        half_ref[w] = jnp.dot(
            left_ref[w, left_id], psi_ref[0], preferred_element_type=F32
        ).astype(BF16)
    for w in range(channels):
        full = jnp.dot(half_ref[w], right_ref[w, right_id], preferred_element_type=F32)
        member = channel_class[x * channels + w]
        before = acc_ref[member]
        acc_ref[member] = jnp.where(first_ref[w] != 0, 0.0, before) + full

    side = lax.rem(step, 2)
    for q in range(4):
        rows = slice(q * EARLY_ROWS, (q + 1) * EARLY_ROWS)
        at = q * quarter
        for h in range(hops):
            stage_ref[side, h, rows] = acc_ref[h + 1, at : at + EARLY_ROWS].astype(BF16)
    for place, q in enumerate(relative_quarters(x)):
        at = pl.multiple_of(q * quarter, quarter)
        own[place, 0] = acc_ref[0, pl.ds(at, quarter)].astype(BF16)
    here, beside, mirror, across = relative_quarters(x)
    orders = ((here, mirror, beside, across), (here, beside, mirror, across))
    start = EARLY_ROWS
    for j, rows in enumerate(CHUNKS):
        for s in range(2):
            keep, send = chunk_outs[4 * j + 2 * s : 4 * j + 2 * s + 2]
            for place, q in enumerate(orders[s]):
                target = keep if place < 2 else send
                at = pl.multiple_of(q * quarter + start, 16)
                for h in range(hops):
                    target[place % 2, h] = acc_ref[
                        h + 1, pl.ds(at, rows), s * LANES : (s + 1) * LANES
                    ].astype(BF16)
        start += rows
    for h in range(hops):
        slot_copy(step, h).start()

    @pl.when(step == pl.num_programs(0) - 1)
    def _():
        for h in range(hops):
            slot_copy(step - 1, h).wait()
        for h in range(hops):
            slot_copy(step, h).wait()
        for i in range(left_count):
            need(left_copy, left_here, i)
        for i in range(right_count):
            need(right_copy, right_here, i)


def products(tables, owners, capacity, psi, left_env, right_env, classes):
    blocks, block, _ = psi.shape
    channels, left_count = left_env.shape[:2]
    right_count = right_env.shape[1]
    quarter = block // 4
    early = 4 * EARLY_ROWS
    hops = classes - 1
    out_shape = [
        pltpu.HBM((4, blocks, quarter, block), BF16),
        pltpu.HBM((owners * capacity, early, block), BF16),
    ]
    out_specs = [
        pl.BlockSpec((4, 1, quarter, block), lambda k, *_: (0, k, 0, 0)),
        pl.BlockSpec(memory_space=pltpu.HBM),
    ]
    for rows in CHUNKS:
        out_shape += [pltpu.HBM((2, blocks * hops, rows, LANES), BF16)] * 4
        out_specs += [pl.BlockSpec((2, hops, rows, LANES), lambda k, *_: (0, k, 0, 0))] * 4
    return pl.pallas_call(
        functools.partial(products_kernel, capacity),
        out_shape=out_shape,
        grid_spec=pltpu.PrefetchScalarGridSpec(
            num_scalar_prefetch=len(tables),
            grid=(blocks,),
            in_specs=[
                pl.BlockSpec((1, block, block), lambda k, *_: (k, 0, 0)),
                pl.BlockSpec(memory_space=pltpu.HBM),
                pl.BlockSpec(memory_space=pltpu.HBM),
            ],
            out_specs=out_specs,
            scratch_shapes=[
                pltpu.VMEM(left_env.shape, BF16),
                pltpu.VMEM(right_env.shape, BF16),
                pltpu.VMEM((channels, block, block), BF16),
                pltpu.VMEM((classes, block, block), F32),
                pltpu.VMEM((2, hops, early, block), BF16),
                pltpu.SMEM((owners,), jnp.int32),
                pltpu.SMEM((channels,), jnp.int32),
                pltpu.SMEM((blocks * hops,), jnp.int32),
                pltpu.SMEM((left_count,), jnp.int32),
                pltpu.SMEM((right_count,), jnp.int32),
                pltpu.SemaphoreType.DMA((left_count,)),
                pltpu.SemaphoreType.DMA((right_count,)),
                pltpu.SemaphoreType.DMA((2, hops)),
            ],
        ),
        compiler_params=pltpu.CompilerParams(vmem_limit_bytes=60 * 2**20),
        cost_estimate=pl.CostEstimate(
            flops=4 * channels * blocks * block**3,
            bytes_accessed=2 * (left_env.size + right_env.size + psi.size * (1 + classes)),
            transcendentals=0,
        ),
        name="products",
    )(*tables, psi, left_env, right_env)


def slots_kernel(items, keep_a, got_a, last_a, keep_b, got_b, last_b, slots):
    def total(keep, got, last, i):
        value = keep[0, i].astype(F32) + got[0, i].astype(F32) + last[i].astype(F32)
        return value.astype(BF16)

    def fill(p, _):
        i = items[p]
        slots[p, :, :LANES] = total(keep_a, got_a, last_a, i)
        slots[p, :, LANES:] = total(keep_b, got_b, last_b, i)
        return 0

    lax.fori_loop(0, slots.shape[0], fill, 0, unroll=4)


def fill_slots(items, parts, final):
    _, count, rows, _ = parts[0].shape
    slot_count = items.shape[0]
    pair = whole((1, count, rows, LANES))
    one = whole((count, rows, LANES))
    return pl.pallas_call(
        slots_kernel,
        out_shape=pltpu.HBM((slot_count, rows, 2 * LANES), BF16),
        grid_spec=pltpu.PrefetchScalarGridSpec(
            num_scalar_prefetch=1,
            grid=(1,),
            in_specs=[pair, pair, one, pair, pair, one],
            out_specs=whole((slot_count, rows, 2 * LANES)),
        ),
        compiler_params=pltpu.CompilerParams(vmem_limit_bytes=60 * 2**20),
        cost_estimate=large_cost() if final else small_cost(),
        name="fill_slots",
    )(items, *parts)


def merge_kernel(device, places, received, own, *rest):
    *outs, acc = rest
    _, blocks, quarter, _ = own.shape
    at = [pl.multiple_of(q * EARLY_ROWS, EARLY_ROWS) for q in relative_quarters(device[0])]
    for p in range(4):
        acc[:blocks, pl.ds(at[p], EARLY_ROWS)] = own[p, :, :EARLY_ROWS].astype(F32)

    def add(p, _):
        acc[places[p]] += received[p].astype(F32)
        return 0

    lax.fori_loop(0, received.shape[0], add, 0, unroll=4)
    for p in range(4):
        outs[p][:, :EARLY_ROWS] = acc[:blocks, pl.ds(at[p], EARLY_ROWS)].astype(BF16)
        outs[p][:, EARLY_ROWS:] = own[p, :, EARLY_ROWS:]


def merge_early(device, places, received, own):
    _, blocks, quarter, width = own.shape
    return pl.pallas_call(
        merge_kernel,
        out_shape=[pltpu.HBM((blocks, quarter, width), BF16)] * 4,
        grid_spec=pltpu.PrefetchScalarGridSpec(
            num_scalar_prefetch=2,
            grid=(1,),
            in_specs=[whole(received.shape), whole(own.shape)],
            out_specs=[whole((blocks, quarter, width))] * 4,
            scratch_shapes=[pltpu.VMEM((blocks + 1, 4 * EARLY_ROWS, width), F32)],
        ),
        compiler_params=pltpu.CompilerParams(vmem_limit_bytes=60 * 2**20),
        cost_estimate=small_cost(),
        name="merge_early",
    )(device, places, received, own)


def add_slots(acc, places, received):
    def add(p, _):
        acc[places[p]] += received[p].astype(F32)
        return 0

    lax.fori_loop(0, received.shape[0], add, 0, unroll=4)


def first_sum(places, received, mine, others, start):
    blocks, quarter, width = mine.shape
    rows = received.shape[1]

    def kernel(places, received, *rest):
        *parts, result, acc = rest

        def total(at):
            value = parts[0][:, at].astype(F32)
            for part in parts[1:]:
                value = value + part[:, at].astype(F32)
            return value

        acc[:blocks] = total(slice(start, start + rows))
        add_slots(acc, places, received)
        result[:, :start] = total(slice(0, start))
        result[:, start : start + rows] = acc[:blocks]
        result[:, start + rows :] = total(slice(start + rows, quarter))

    return pl.pallas_call(
        kernel,
        out_shape=pltpu.HBM(mine.shape, F32),
        grid_spec=pltpu.PrefetchScalarGridSpec(
            num_scalar_prefetch=1,
            grid=(1,),
            in_specs=[whole(received.shape)] + [whole(mine.shape)] * (1 + len(others)),
            out_specs=whole(mine.shape),
            scratch_shapes=[pltpu.VMEM((blocks + 1, rows, width), F32)],
        ),
        compiler_params=pltpu.CompilerParams(vmem_limit_bytes=60 * 2**20),
        cost_estimate=large_cost(),
        name="first_sum",
    )(places, received, mine, *others)


def last_sum(places, received, so_far, start):
    blocks, _, width = so_far.shape
    rows = received.shape[1]
    part = pl.BlockSpec((blocks, rows, width), lambda i, *_: (0, start // rows, 0))

    def kernel(places, received, so_far, result, acc):
        acc[:blocks] = so_far[...]
        add_slots(acc, places, received)
        result[...] = acc[:blocks]

    return pl.pallas_call(
        kernel,
        out_shape=pltpu.HBM(so_far.shape, F32),
        grid_spec=pltpu.PrefetchScalarGridSpec(
            num_scalar_prefetch=1,
            grid=(1,),
            in_specs=[whole(received.shape), part],
            out_specs=part,
            scratch_shapes=[pltpu.VMEM((blocks + 1, rows, width), F32)],
        ),
        input_output_aliases={2: 0},
        compiler_params=pltpu.CompilerParams(vmem_limit_bytes=60 * 2**20),
        cost_estimate=small_cost(),
        name="last_sum",
    )(places, received, so_far)


def item_places(targets, block_count):
    destined = targets // block_count
    count = targets.shape[-1]
    earlier = jnp.arange(count)[:, None] > jnp.arange(count)[None, :]
    same = (destined[..., :, None] == destined[..., None, :]) & earlier
    return destined, jnp.sum(same.astype(jnp.int32), axis=-1)


def shards(wavefunction, left_env, right_env, block_left, block_right, channel_class, hop_target):
    block_count = wavefunction.shape[0]
    hop_count = hop_target.shape[1]
    owners = lax.axis_size("lsec") * lax.axis_size("rsec")
    item_count = block_count * hop_count
    capacity = 2 * ((item_count + owners - 1) // owners)
    slot_count = owners * capacity
    me = lax.axis_index("lsec") * lax.axis_size("rsec") + lax.axis_index("rsec")
    device = jnp.stack([lax.axis_index(axis) for axis in ("mpo", "lsec", "rsec")]).astype(jnp.int32)
    targets = hop_target.reshape(owners, item_count)
    own_targets = lax.dynamic_index_in_dim(targets, me, 0, False)
    own, early_slots, *parts = products(
        (device, block_left, block_right, channel_class, own_targets),
        owners,
        capacity,
        wavefunction,
        left_env,
        right_env,
        hop_count + 1,
    )

    destined, slot = item_places(own_targets, block_count)
    position = destined * capacity + slot
    held = position[:, None] == jnp.arange(slot_count, dtype=jnp.int32)[None, :]
    index = jnp.arange(item_count, dtype=jnp.int32)
    slot_items = jnp.sum(jnp.where(held, index[:, None], 0), axis=0)
    destined_all, slot_all = item_places(targets, block_count)
    mine = (destined_all == me)[:, :, None] & (
        slot_all[:, :, None] == jnp.arange(capacity, dtype=jnp.int32)
    )
    local = targets - (me + 1) * block_count
    places = jnp.sum(jnp.where(mine, local[:, :, None], 0), axis=1).reshape(slot_count)
    places = places + block_count

    beside = [(i, i ^ 1) for i in range(4)]
    mirror = [(i, 3 - i) for i in range(4)]
    across = [(i, (i + 2) % 4) for i in range(4)]

    def second(keep, got):
        return (keep[1].astype(F32) + got[1].astype(F32)).astype(BF16)

    early = lax.all_to_all(early_slots, ("lsec", "rsec"), 0, 0, tiled=True)
    got, last = [], []
    for j in range(len(CHUNKS)):
        keep_a, send_a, keep_b, send_b = parts[4 * j : 4 * j + 4]
        got.append((lax.ppermute(send_a, "mpo", beside), lax.ppermute(send_b, "mpo", mirror)))
    for j in range(len(CHUNKS)):
        keep_a, _, keep_b, _ = parts[4 * j : 4 * j + 4]
        got_a, got_b = got[j]
        if j > 0:
            got_a, got_b, *last[j - 1] = lax.optimization_barrier((got_a, got_b, *last[j - 1]))
        then_a, then_b = lax.optimization_barrier((second(keep_a, got_a), second(keep_b, got_b)))
        last.append([lax.ppermute(then_a, "mpo", mirror), lax.ppermute(then_b, "mpo", beside)])

    def send(j, last_a, last_b):
        keep_a, _, keep_b, _ = parts[4 * j : 4 * j + 4]
        group = (keep_a, got[j][0], last_a, keep_b, got[j][1], last_b)
        return fill_slots(slot_items, group, j + 1 == len(CHUNKS))

    last_a, last_b, early, then_a, then_b = lax.optimization_barrier(
        (*last[0], early, then_a, then_b)
    )
    slots = send(0, last_a, last_b)
    early, slots = lax.optimization_barrier((early, slots))
    received = lax.all_to_all(slots, ("lsec", "rsec"), 0, 0, tiled=True)
    out_mine, *out_others = merge_early(device, places, early, own)
    others = [
        lax.ppermute(part, "mpo", pairs)
        for part, pairs in zip(out_others, (beside, mirror, across))
    ]
    slots = send(1, *last[1])
    received_last = lax.all_to_all(slots, ("lsec", "rsec"), 0, 0, tiled=True)
    base = first_sum(places, received, out_mine, others, EARLY_ROWS)
    return last_sum(places, received_last, base, EARLY_ROWS + CHUNKS[0])


def solution(mesh):
    in_specs = (
        P(("lsec", "rsec"), None, None),
        P("mpo", "lsec", None, None),
        P("mpo", "rsec", None, None),
        P(("lsec", "rsec")),
        P(("lsec", "rsec")),
        P(),
        P(),
    )
    out_specs = P(("lsec", "rsec"), "mpo", None)
    return jax.shard_map(shards, mesh=mesh, in_specs=in_specs, out_specs=out_specs, check_vma=False)
```

```python
import functools

import jax
import jax.numpy as jnp
from jax import lax
from jax.experimental import pallas as pl
from jax.experimental.pallas import tpu as pltpu
from jax.sharding import PartitionSpec as P

LANES = 128
EARLY_ROWS = 16
CHUNKS = (16, 32)
SIDES = 2
HEAD = 3
AHEAD = 2
BF16 = jnp.bfloat16
F32 = jnp.float32


SMALL_VMEM = 20 * 2**20
IN_VMEM = pl.BlockSpec(memory_space=pltpu.VMEM)


def small_cost():
    return pl.CostEstimate(flops=1, bytes_accessed=1, transcendentals=0)


def large_cost():
    return pl.CostEstimate(flops=6 * 10**10, bytes_accessed=1, transcendentals=0)


def whole(shape):
    return pl.BlockSpec(shape, lambda i, *_: (0,) * len(shape))


def relative_quarters(x):
    return x, x ^ 1, 3 - x, (3 - x) ^ 1


def products_kernel(
    capacity, device, block_left, block_right, channel_class, own_targets, psi_hbm, left_hbm,
    right_hbm, own, slots_hbm, *rest
):
    chunk_outs = rest[: 4 * len(CHUNKS)]
    (
        psi_ref, left_ref, right_ref, half_ref, acc_ref, stage_ref, seen_ref, first_ref, empty_ref,
        slot_ref, psi_sems, left_sems, right_sems, slot_sems,
    ) = rest[4 * len(CHUNKS) :]
    channels, left_count, _, _ = left_ref.shape
    right_count = right_ref.shape[1]
    classes = acc_ref.shape[1]
    hops = classes - 1
    quarter = acc_ref.shape[2] // 4
    head = SIDES * HEAD
    step = pl.program_id(0)
    steps = pl.num_programs(0)
    blocks = SIDES * steps
    x = device[0]

    def psi_copy(part):
        at = pl.ds(0, head) if part == 0 else pl.ds(head, psi_ref.shape[0] - head)
        return pltpu.make_async_copy(psi_hbm.at[at], psi_ref.at[at], psi_sems.at[part])

    def left_copy(w):
        return pltpu.make_async_copy(left_hbm.at[w], left_ref.at[w], left_sems.at[w])

    def right_copy(w):
        return pltpu.make_async_copy(right_hbm.at[w], right_ref.at[w], right_sems.at[w])

    def slot_copy(turn, side, h):
        flip = lax.rem(turn, 2)
        k = SIDES * turn + side
        return pltpu.make_async_copy(
            stage_ref.at[flip, side, h],
            slots_hbm.at[slot_ref[k * hops + h]],
            slot_sems.at[flip, side, h],
        )

    def each_slot(turn, act):
        for side in range(SIDES):
            for h in range(hops):
                act(slot_copy(turn, side, h))

    def sectors(k):
        return (
            block_left[k] - device[1] * left_count,
            block_right[k] - device[2] * right_count,
        )

    def first_product(w, k, left_id, place):
        half_ref[place] = jnp.dot(
            left_ref[w, left_id], psi_ref[k], preferred_element_type=F32
        ).astype(BF16)

    def second_product(w, right_id, place, at):
        full = jnp.dot(half_ref[place], right_ref[w, right_id], preferred_element_type=F32)
        member = channel_class[x * channels + w]
        before = acc_ref[at, member]
        acc_ref[at, member] = jnp.where(first_ref[w] != 0, 0.0, before) + full

    def emit_parts():
        flip = lax.rem(step, 2)
        here, beside, mirror, across = relative_quarters(x)
        orders = ((here, mirror, beside, across), (here, beside, mirror, across))

        def early_part(side, at, h):
            for q in range(4):
                rows = slice(q * EARLY_ROWS, (q + 1) * EARLY_ROWS)
                first = q * quarter
                stage_ref[flip, side, h, rows] = acc_ref[
                    at, h + 1, first : first + EARLY_ROWS
                ].astype(BF16)

        def own_part(side, at, place, q):
            row = pl.multiple_of(q * quarter, quarter)
            own[place, side] = acc_ref[at, 0, pl.ds(row, quarter)].astype(BF16)

        def chunk_part(side, at, h, j, start, rows, s):
            keep, send = chunk_outs[4 * j + 2 * s : 4 * j + 2 * s + 2]
            for place, q in enumerate(orders[s]):
                target = keep if place < 2 else send
                row = pl.multiple_of(q * quarter + start, 16)
                target[place % 2, side * hops + h] = acc_ref[
                    at, h + 1, pl.ds(row, rows), s * LANES : (s + 1) * LANES
                ].astype(BF16)

        work = []
        for side in range(SIDES):
            at = SIDES * lax.rem(step, HEAD) + side
            for h in range(hops):
                work.append(functools.partial(early_part, side, at, h))
            for place, q in enumerate((here, beside, mirror, across)):
                work.append(functools.partial(own_part, side, at, place, q))
            start = EARLY_ROWS
            for j, rows in enumerate(CHUNKS):
                for s in range(2):
                    for h in range(hops):
                        work.append(
                            functools.partial(chunk_part, side, at, h, j, start, rows, s)
                        )
                start += rows
        return work

    @pl.when(step == 0)
    def _():
        psi_copy(0).start()
        for w in range(AHEAD):
            left_copy(w).start()
            right_copy(w).start()
        for i in range(seen_ref.shape[0]):
            seen_ref[i] = 0

        def place(i, _):
            owner = lax.div(own_targets[i], blocks)
            earlier = seen_ref[owner]
            slot_ref[i] = owner * capacity + earlier
            seen_ref[owner] = earlier + 1
            return 0

        lax.fori_loop(0, slot_ref.shape[0], place, 0)
        for c in range(classes):
            empty_ref[c] = 1
        for w in range(channels):
            member = channel_class[x * channels + w]
            first_ref[w] = empty_ref[member]
            empty_ref[member] = 0
        for c in range(classes):

            @pl.when(empty_ref[c] != 0)
            def _():
                for at in range(head):
                    acc_ref[at, c] = jnp.zeros(acc_ref.shape[2:], F32)

        psi_copy(0).wait()

        def channel(w, _):
            left_copy(w).wait()
            right_copy(w).wait()

            @pl.when(w + AHEAD < channels)
            def _():
                left_copy(w + AHEAD).start()
                right_copy(w + AHEAD).start()

            @pl.when(w + AHEAD == channels)
            def _():
                psi_copy(1).start()

            ids = [sectors(k) for k in range(head)]
            for k in range(head):
                first_product(w, k, ids[k][0], k)
            for k in range(head):
                second_product(w, ids[k][1], k, k)
            return 0

        lax.fori_loop(0, channels, channel, 0)
        for part in emit_parts():
            part()

    @pl.when(step == 1)
    def _():
        psi_copy(1).wait()

    @pl.when(step >= 2)
    def _():
        each_slot(step - 2, lambda copy: copy.wait())

    @pl.when((step > 0) & (step <= steps - HEAD))
    def _():
        work = emit_parts()
        turns = SIDES * channels
        pair = step + HEAD - 1
        for side in range(SIDES):
            k = SIDES * pair + side
            left_id, right_id = sectors(k)
            at = SIDES * lax.rem(pair, HEAD) + side
            for w in range(channels):
                first_product(w, k, left_id, side * channels + w)
            for w in range(channels):
                second_product(w, right_id, side * channels + w, at)
                turn = side * channels + w
                for part in work[turn * len(work) // turns : (turn + 1) * len(work) // turns]:
                    part()

    @pl.when(step > steps - HEAD)
    def _():
        for part in emit_parts():
            part()

    each_slot(step, lambda copy: copy.start())

    @pl.when(step == steps - 1)
    def _():
        each_slot(step - 1, lambda copy: copy.wait())
        each_slot(step, lambda copy: copy.wait())


def products(tables, owners, capacity, psi, left_env, right_env, classes):
    blocks, block, _ = psi.shape
    channels = left_env.shape[0]
    quarter = block // 4
    early = 4 * EARLY_ROWS
    hops = classes - 1
    head = SIDES * HEAD
    out_shape = [
        pltpu.HBM((4, blocks, quarter, block), BF16),
        pltpu.HBM((owners * capacity, early, block), BF16),
    ]
    out_specs = [
        pl.BlockSpec((4, SIDES, quarter, block), lambda k, *_: (0, k, 0, 0)),
        pl.BlockSpec(memory_space=pltpu.HBM),
    ]
    for rows in CHUNKS:
        out_shape += [pltpu.HBM((2, blocks * hops, rows, LANES), BF16)] * 4
        block_shape = (2, SIDES * hops, rows, LANES)
        out_specs += [pl.BlockSpec(block_shape, lambda k, *_: (0, k, 0, 0))] * 4
    return pl.pallas_call(
        functools.partial(products_kernel, capacity),
        out_shape=out_shape,
        grid_spec=pltpu.PrefetchScalarGridSpec(
            num_scalar_prefetch=len(tables),
            grid=(blocks // SIDES,),
            in_specs=[pl.BlockSpec(memory_space=pltpu.HBM)] * 3,
            out_specs=out_specs,
            scratch_shapes=[
                pltpu.VMEM(psi.shape, BF16),
                pltpu.VMEM(left_env.shape, BF16),
                pltpu.VMEM(right_env.shape, BF16),
                pltpu.VMEM((max(head, SIDES * channels), block, block), BF16),
                pltpu.VMEM((head, classes, block, block), F32),
                pltpu.VMEM((2, SIDES, hops, early, block), BF16),
                pltpu.SMEM((owners,), jnp.int32),
                pltpu.SMEM((channels,), jnp.int32),
                pltpu.SMEM((classes,), jnp.int32),
                pltpu.SMEM((blocks * hops,), jnp.int32),
                pltpu.SemaphoreType.DMA((2,)),
                pltpu.SemaphoreType.DMA((channels,)),
                pltpu.SemaphoreType.DMA((channels,)),
                pltpu.SemaphoreType.DMA((2, SIDES, hops)),
            ],
        ),
        compiler_params=pltpu.CompilerParams(vmem_limit_bytes=60 * 2**20),
        cost_estimate=pl.CostEstimate(
            flops=4 * channels * blocks * block**3,
            bytes_accessed=2 * (left_env.size + right_env.size + psi.size * (1 + classes)),
            transcendentals=0,
        ),
        name="products",
    )(*tables, psi, left_env, right_env)


def slots_kernel(positions, keep_a, got_a, last_a, keep_b, got_b, last_b, slots, stage, sems):
    def total(keep, got, last, i):
        value = keep[0, i].astype(F32) + got[0, i].astype(F32) + last[i].astype(F32)
        return value.astype(BF16)

    def copy(i):
        return pltpu.make_async_copy(stage.at[i], slots.at[positions[i]], sems.at[i])

    def fill(i, _):
        stage[i, :, :LANES] = total(keep_a, got_a, last_a, i)
        stage[i, :, LANES:] = total(keep_b, got_b, last_b, i)
        copy(i).start()
        return 0

    def finish(i, _):
        copy(i).wait()
        return 0

    lax.fori_loop(0, stage.shape[0], fill, 0, unroll=4)
    lax.fori_loop(0, stage.shape[0], finish, 0, unroll=4)


def fill_slots(positions, slot_count, parts, final):
    _, count, rows, _ = parts[0].shape
    return pl.pallas_call(
        slots_kernel,
        out_shape=pltpu.HBM((slot_count, rows, 2 * LANES), BF16),
        grid_spec=pltpu.PrefetchScalarGridSpec(
            num_scalar_prefetch=1,
            grid=(1,),
            in_specs=[IN_VMEM] * 6,
            out_specs=pl.BlockSpec(memory_space=pltpu.HBM),
            scratch_shapes=[
                pltpu.VMEM((count, rows, 2 * LANES), BF16),
                pltpu.SemaphoreType.DMA((count,)),
            ],
        ),
        compiler_params=pltpu.CompilerParams(vmem_limit_bytes=SMALL_VMEM),
        cost_estimate=large_cost() if final else small_cost(),
        name="fill_slots",
    )(positions, *parts)


def merge_kernel(device, places, received, own, *rest):
    *outs, acc = rest
    _, blocks, quarter, _ = own.shape
    at = [pl.multiple_of(q * EARLY_ROWS, EARLY_ROWS) for q in relative_quarters(device[0])]
    for p in range(4):
        acc[:blocks, pl.ds(at[p], EARLY_ROWS)] = own[p, :, :EARLY_ROWS].astype(F32)

    def add(p, _):
        acc[places[p]] += received[p].astype(F32)
        return 0

    lax.fori_loop(0, received.shape[0], add, 0, unroll=4)
    for p in range(4):
        outs[p][:, :EARLY_ROWS] = acc[:blocks, pl.ds(at[p], EARLY_ROWS)].astype(BF16)
        outs[p][:, EARLY_ROWS:] = own[p, :, EARLY_ROWS:]


def merge_early(device, places, received, own):
    _, blocks, quarter, width = own.shape
    return pl.pallas_call(
        merge_kernel,
        out_shape=[pltpu.HBM((blocks, quarter, width), BF16)] * 4,
        grid_spec=pltpu.PrefetchScalarGridSpec(
            num_scalar_prefetch=2,
            grid=(1,),
            in_specs=[IN_VMEM, IN_VMEM],
            out_specs=[whole((blocks, quarter, width))] * 4,
            scratch_shapes=[pltpu.VMEM((blocks + 1, 4 * EARLY_ROWS, width), F32)],
        ),
        compiler_params=pltpu.CompilerParams(vmem_limit_bytes=SMALL_VMEM),
        cost_estimate=small_cost(),
        name="merge_early",
    )(device, places, received, own)


def add_slots(acc, places, received):
    def add(p, _):
        acc[places[p]] += received[p].astype(F32)
        return 0

    lax.fori_loop(0, received.shape[0], add, 0, unroll=4)


def first_sum(places, received, mine, others, start):
    blocks, quarter, width = mine.shape
    rows = received.shape[1]

    def kernel(places, received, *rest):
        *parts, result, acc = rest

        def total(at):
            value = parts[0][:, at].astype(F32)
            for part in parts[1:]:
                value = value + part[:, at].astype(F32)
            return value

        acc[:blocks] = total(slice(start, start + rows))
        add_slots(acc, places, received)
        result[:, :start] = total(slice(0, start))
        result[:, start : start + rows] = acc[:blocks]
        result[:, start + rows :] = total(slice(start + rows, quarter))

    return pl.pallas_call(
        kernel,
        out_shape=pltpu.HBM(mine.shape, F32),
        grid_spec=pltpu.PrefetchScalarGridSpec(
            num_scalar_prefetch=1,
            grid=(1,),
            in_specs=[IN_VMEM] * (2 + len(others)),
            out_specs=whole(mine.shape),
            scratch_shapes=[pltpu.VMEM((blocks + 1, rows, width), F32)],
        ),
        compiler_params=pltpu.CompilerParams(vmem_limit_bytes=SMALL_VMEM),
        cost_estimate=large_cost(),
        name="first_sum",
    )(places, received, mine, *others)


def last_sum(places, received, so_far, start):
    blocks, _, width = so_far.shape
    rows = received.shape[1]
    part = pl.BlockSpec((blocks, rows, width), lambda i, *_: (0, start // rows, 0))

    def kernel(places, received, so_far, result, acc):
        acc[:blocks] = so_far[...]
        add_slots(acc, places, received)
        result[...] = acc[:blocks]

    return pl.pallas_call(
        kernel,
        out_shape=pltpu.HBM(so_far.shape, F32),
        grid_spec=pltpu.PrefetchScalarGridSpec(
            num_scalar_prefetch=1,
            grid=(1,),
            in_specs=[IN_VMEM, part],
            out_specs=part,
            scratch_shapes=[pltpu.VMEM((blocks + 1, rows, width), F32)],
        ),
        input_output_aliases={2: 0},
        compiler_params=pltpu.CompilerParams(vmem_limit_bytes=SMALL_VMEM),
        cost_estimate=small_cost(),
        name="last_sum",
    )(places, received, so_far)


def item_places(targets, block_count):
    destined = targets // block_count
    count = targets.shape[-1]
    earlier = jnp.arange(count)[:, None] > jnp.arange(count)[None, :]
    same = (destined[..., :, None] == destined[..., None, :]) & earlier
    return destined, jnp.sum(same.astype(jnp.int32), axis=-1)


def shards(wavefunction, left_env, right_env, block_left, block_right, channel_class, hop_target):
    block_count = wavefunction.shape[0]
    hop_count = hop_target.shape[1]
    owners = lax.axis_size("lsec") * lax.axis_size("rsec")
    item_count = block_count * hop_count
    capacity = 2 * ((item_count + owners - 1) // owners)
    slot_count = owners * capacity
    me = lax.axis_index("lsec") * lax.axis_size("rsec") + lax.axis_index("rsec")
    device = jnp.stack([lax.axis_index(axis) for axis in ("mpo", "lsec", "rsec")]).astype(jnp.int32)
    targets = hop_target.reshape(owners, item_count)
    own_targets = lax.dynamic_index_in_dim(targets, me, 0, False)
    own, early_slots, *parts = products(
        (device, block_left, block_right, channel_class, own_targets),
        owners,
        capacity,
        wavefunction,
        left_env,
        right_env,
        hop_count + 1,
    )

    destined, slot = item_places(own_targets, block_count)
    position = destined * capacity + slot
    destined_all, slot_all = item_places(targets, block_count)
    mine = (destined_all == me)[:, :, None] & (
        slot_all[:, :, None] == jnp.arange(capacity, dtype=jnp.int32)
    )
    local = targets - (me + 1) * block_count
    places = jnp.sum(jnp.where(mine, local[:, :, None], 0), axis=1).reshape(slot_count)
    places = places + block_count

    beside = [(i, i ^ 1) for i in range(4)]
    mirror = [(i, 3 - i) for i in range(4)]
    across = [(i, (i + 2) % 4) for i in range(4)]

    def second(keep, got):
        return (keep[1].astype(F32) + got[1].astype(F32)).astype(BF16)

    early = lax.all_to_all(early_slots, ("lsec", "rsec"), 0, 0, tiled=True)
    got, last = [], []
    for j in range(len(CHUNKS)):
        keep_a, send_a, keep_b, send_b = parts[4 * j : 4 * j + 4]
        got.append((lax.ppermute(send_a, "mpo", beside), lax.ppermute(send_b, "mpo", mirror)))
    for j in range(len(CHUNKS)):
        keep_a, _, keep_b, _ = parts[4 * j : 4 * j + 4]
        got_a, got_b = got[j]
        if j > 0:
            got_a, got_b, *last[j - 1] = lax.optimization_barrier((got_a, got_b, *last[j - 1]))
        then_a, then_b = lax.optimization_barrier((second(keep_a, got_a), second(keep_b, got_b)))
        last.append([lax.ppermute(then_a, "mpo", mirror), lax.ppermute(then_b, "mpo", beside)])

    def send(j, last_a, last_b):
        keep_a, _, keep_b, _ = parts[4 * j : 4 * j + 4]
        group = (keep_a, got[j][0], last_a, keep_b, got[j][1], last_b)
        return fill_slots(position, slot_count, group, j + 1 == len(CHUNKS))

    last_a, last_b, then_a, then_b = lax.optimization_barrier((*last[0], then_a, then_b))
    slots = send(0, last_a, last_b)
    early, slots = lax.optimization_barrier((early, slots))
    received = lax.all_to_all(slots, ("lsec", "rsec"), 0, 0, tiled=True)
    out_mine, *out_others = merge_early(device, places, early, own)
    slots = send(1, *last[1])
    out_others, slots = lax.optimization_barrier((out_others, slots))
    others = [
        lax.ppermute(part, "mpo", pairs)
        for part, pairs in zip(out_others, (beside, mirror, across))
    ]
    received_last = lax.all_to_all(slots, ("lsec", "rsec"), 0, 0, tiled=True)
    base = first_sum(places, received, out_mine, others, EARLY_ROWS)
    return last_sum(places, received_last, base, EARLY_ROWS + CHUNKS[0])


def solution(mesh):
    in_specs = (
        P(("lsec", "rsec"), None, None),
        P("mpo", "lsec", None, None),
        P("mpo", "rsec", None, None),
        P(("lsec", "rsec")),
        P(("lsec", "rsec")),
        P(),
        P(),
    )
    out_specs = P(("lsec", "rsec"), "mpo", None)
    return jax.shard_map(shards, mesh=mesh, in_specs=in_specs, out_specs=out_specs, check_vma=False)
```

```python
import functools

import jax
import jax.numpy as jnp
from jax import lax
from jax.experimental import pallas as pl
from jax.experimental.pallas import tpu as pltpu
from jax.sharding import PartitionSpec as P

LANES = 128
EARLY_ROWS = 16
CHUNKS = (48,)
FILL_FLOPS = 3 * 10**10
SIDES = 2
HEAD = 3
AHEAD = 2
BF16 = jnp.bfloat16
F32 = jnp.float32


SMALL_VMEM = 20 * 2**20
IN_VMEM = pl.BlockSpec(memory_space=pltpu.VMEM)


def cost(flops=1):
    return pl.CostEstimate(flops=flops, bytes_accessed=1, transcendentals=0)


def whole(shape):
    return pl.BlockSpec(shape, lambda i, *_: (0,) * len(shape))


def relative_quarters(x):
    return x, x ^ 1, 3 - x, (3 - x) ^ 1


def products_kernel(
    capacity, device, block_left, block_right, channel_class, own_targets, psi_hbm, left_hbm,
    right_hbm, own_early, slots_hbm, *rest
):
    own_late = rest[:4]
    chunk_outs = rest[4 : 4 + 4 * len(CHUNKS)]
    (
        psi_ref, left_ref, right_ref, half_ref, acc_ref, stage_ref, seen_ref, first_ref, empty_ref,
        slot_ref, psi_sems, left_sems, right_sems, slot_sems,
    ) = rest[4 + 4 * len(CHUNKS) :]
    channels, left_count, _, _ = left_ref.shape
    right_count = right_ref.shape[1]
    classes = acc_ref.shape[1]
    hops = classes - 1
    quarter = acc_ref.shape[2] // 4
    head = SIDES * HEAD
    step = pl.program_id(0)
    steps = pl.num_programs(0)
    blocks = SIDES * steps
    x = device[0]

    def psi_copy(part):
        at = pl.ds(0, head) if part == 0 else pl.ds(head, psi_ref.shape[0] - head)
        return pltpu.make_async_copy(psi_hbm.at[at], psi_ref.at[at], psi_sems.at[part])

    def left_copy(w):
        return pltpu.make_async_copy(left_hbm.at[w], left_ref.at[w], left_sems.at[w])

    def right_copy(w):
        return pltpu.make_async_copy(right_hbm.at[w], right_ref.at[w], right_sems.at[w])

    def slot_copy(turn, side, h):
        flip = lax.rem(turn, 2)
        k = SIDES * turn + side
        return pltpu.make_async_copy(
            stage_ref.at[flip, side, h],
            slots_hbm.at[slot_ref[k * hops + h]],
            slot_sems.at[flip, side, h],
        )

    def each_slot(turn, act):
        for side in range(SIDES):
            for h in range(hops):
                act(slot_copy(turn, side, h))

    def sectors(k):
        return (
            block_left[k] - device[1] * left_count,
            block_right[k] - device[2] * right_count,
        )

    def first_product(w, k, left_id, place):
        half_ref[place] = jnp.dot(
            left_ref[w, left_id], psi_ref[k], preferred_element_type=F32
        ).astype(BF16)

    def second_product(w, right_id, place, at):
        full = jnp.dot(half_ref[place], right_ref[w, right_id], preferred_element_type=F32)
        member = channel_class[x * channels + w]
        before = acc_ref[at, member]
        acc_ref[at, member] = jnp.where(first_ref[w] != 0, 0.0, before) + full

    def emit_parts():
        flip = lax.rem(step, 2)
        here, beside, mirror, across = relative_quarters(x)
        orders = ((here, mirror, beside, across), (here, beside, mirror, across))

        def early_part(side, at, h):
            for q in range(4):
                rows = slice(q * EARLY_ROWS, (q + 1) * EARLY_ROWS)
                first = q * quarter
                stage_ref[flip, side, h, rows] = acc_ref[
                    at, h + 1, first : first + EARLY_ROWS
                ].astype(BF16)

        def own_part(side, at, place, q):
            row = pl.multiple_of(q * quarter, quarter)
            own_early[place, side] = acc_ref[at, 0, pl.ds(row, EARLY_ROWS)].astype(BF16)
            row = pl.multiple_of(row + EARLY_ROWS, EARLY_ROWS)
            own_late[place][side] = acc_ref[at, 0, pl.ds(row, quarter - EARLY_ROWS)].astype(BF16)

        def chunk_part(side, at, h, j, start, rows, s):
            keep, send = chunk_outs[4 * j + 2 * s : 4 * j + 2 * s + 2]
            for place, q in enumerate(orders[s]):
                target = keep if place < 2 else send
                row = pl.multiple_of(q * quarter + start, 16)
                target[place % 2, side * hops + h] = acc_ref[
                    at, h + 1, pl.ds(row, rows), s * LANES : (s + 1) * LANES
                ].astype(BF16)

        work = []
        for side in range(SIDES):
            at = SIDES * lax.rem(step, HEAD) + side
            for h in range(hops):
                work.append(functools.partial(early_part, side, at, h))
            for place, q in enumerate((here, beside, mirror, across)):
                work.append(functools.partial(own_part, side, at, place, q))
            start = EARLY_ROWS
            for j, rows in enumerate(CHUNKS):
                for s in range(2):
                    for h in range(hops):
                        work.append(
                            functools.partial(chunk_part, side, at, h, j, start, rows, s)
                        )
                start += rows
        return work

    @pl.when(step == 0)
    def _():
        psi_copy(0).start()
        for w in range(AHEAD):
            left_copy(w).start()
            right_copy(w).start()
        for i in range(seen_ref.shape[0]):
            seen_ref[i] = 0

        def place(i, _):
            owner = lax.div(own_targets[i], blocks)
            earlier = seen_ref[owner]
            slot_ref[i] = owner * capacity + earlier
            seen_ref[owner] = earlier + 1
            return 0

        lax.fori_loop(0, slot_ref.shape[0], place, 0)
        for c in range(classes):
            empty_ref[c] = 1
        for w in range(channels):
            member = channel_class[x * channels + w]
            first_ref[w] = empty_ref[member]
            empty_ref[member] = 0
        for c in range(classes):

            @pl.when(empty_ref[c] != 0)
            def _():
                for at in range(head):
                    acc_ref[at, c] = jnp.zeros(acc_ref.shape[2:], F32)

        psi_copy(0).wait()

        def channel(w, _):
            left_copy(w).wait()
            right_copy(w).wait()

            @pl.when(w + AHEAD < channels)
            def _():
                left_copy(w + AHEAD).start()
                right_copy(w + AHEAD).start()

            @pl.when(w + AHEAD == channels)
            def _():
                psi_copy(1).start()

            ids = [sectors(k) for k in range(head)]
            for k in range(head):
                first_product(w, k, ids[k][0], k)
            for k in range(head):
                second_product(w, ids[k][1], k, k)
            return 0

        lax.fori_loop(0, channels, channel, 0)
        for part in emit_parts():
            part()

    @pl.when(step == 1)
    def _():
        psi_copy(1).wait()

    @pl.when(step >= 2)
    def _():
        each_slot(step - 2, lambda copy: copy.wait())

    @pl.when((step > 0) & (step <= steps - HEAD))
    def _():
        work = emit_parts()
        turns = SIDES * channels
        pair = step + HEAD - 1
        for side in range(SIDES):
            k = SIDES * pair + side
            left_id, right_id = sectors(k)
            at = SIDES * lax.rem(pair, HEAD) + side
            for w in range(channels):
                first_product(w, k, left_id, side * channels + w)
            for w in range(channels):
                second_product(w, right_id, side * channels + w, at)
                turn = side * channels + w
                for part in work[turn * len(work) // turns : (turn + 1) * len(work) // turns]:
                    part()

    @pl.when(step > steps - HEAD)
    def _():
        for part in emit_parts():
            part()

    each_slot(step, lambda copy: copy.start())

    @pl.when(step == steps - 1)
    def _():
        each_slot(step - 1, lambda copy: copy.wait())
        each_slot(step, lambda copy: copy.wait())


def products(tables, owners, capacity, psi, left_env, right_env, classes):
    blocks, block, _ = psi.shape
    channels = left_env.shape[0]
    quarter = block // 4
    early = 4 * EARLY_ROWS
    hops = classes - 1
    head = SIDES * HEAD
    out_shape = [
        pltpu.HBM((4, blocks, EARLY_ROWS, block), BF16),
        pltpu.HBM((owners * capacity, early, block), BF16),
    ] + [pltpu.HBM((blocks, quarter - EARLY_ROWS, block), BF16)] * 4
    out_specs = [
        pl.BlockSpec((4, SIDES, EARLY_ROWS, block), lambda k, *_: (0, k, 0, 0)),
        pl.BlockSpec(memory_space=pltpu.HBM),
    ] + [pl.BlockSpec((SIDES, quarter - EARLY_ROWS, block), lambda k, *_: (k, 0, 0))] * 4
    for rows in CHUNKS:
        out_shape += [pltpu.HBM((2, blocks * hops, rows, LANES), BF16)] * 4
        block_shape = (2, SIDES * hops, rows, LANES)
        out_specs += [pl.BlockSpec(block_shape, lambda k, *_: (0, k, 0, 0))] * 4
    return pl.pallas_call(
        functools.partial(products_kernel, capacity),
        out_shape=out_shape,
        grid_spec=pltpu.PrefetchScalarGridSpec(
            num_scalar_prefetch=len(tables),
            grid=(blocks // SIDES,),
            in_specs=[pl.BlockSpec(memory_space=pltpu.HBM)] * 3,
            out_specs=out_specs,
            scratch_shapes=[
                pltpu.VMEM(psi.shape, BF16),
                pltpu.VMEM(left_env.shape, BF16),
                pltpu.VMEM(right_env.shape, BF16),
                pltpu.VMEM((max(head, SIDES * channels), block, block), BF16),
                pltpu.VMEM((head, classes, block, block), F32),
                pltpu.VMEM((2, SIDES, hops, early, block), BF16),
                pltpu.SMEM((owners,), jnp.int32),
                pltpu.SMEM((channels,), jnp.int32),
                pltpu.SMEM((classes,), jnp.int32),
                pltpu.SMEM((blocks * hops,), jnp.int32),
                pltpu.SemaphoreType.DMA((2,)),
                pltpu.SemaphoreType.DMA((channels,)),
                pltpu.SemaphoreType.DMA((channels,)),
                pltpu.SemaphoreType.DMA((2, SIDES, hops)),
            ],
        ),
        compiler_params=pltpu.CompilerParams(vmem_limit_bytes=60 * 2**20),
        cost_estimate=pl.CostEstimate(
            flops=4 * channels * blocks * block**3,
            bytes_accessed=2 * (left_env.size + right_env.size + psi.size * (1 + classes)),
            transcendentals=0,
        ),
        name="products",
    )(*tables, psi, left_env, right_env)


def slots_kernel(positions, keep_a, got_a, last_a, keep_b, got_b, last_b, slots, stage, sems):
    def total(keep, got, last, i):
        value = keep[0, i].astype(F32) + got[0, i].astype(F32) + last[i].astype(F32)
        return value.astype(BF16)

    def copy(i):
        return pltpu.make_async_copy(stage.at[i], slots.at[positions[i]], sems.at[i])

    def fill(i, _):
        stage[i, :, :LANES] = total(keep_a, got_a, last_a, i)
        stage[i, :, LANES:] = total(keep_b, got_b, last_b, i)
        copy(i).start()
        return 0

    def finish(i, _):
        copy(i).wait()
        return 0

    lax.fori_loop(0, stage.shape[0], fill, 0, unroll=4)
    lax.fori_loop(0, stage.shape[0], finish, 0, unroll=4)


def fill_slots(positions, slot_count, parts):
    _, count, rows, _ = parts[0].shape
    pair = whole((1, count, rows, LANES))
    return pl.pallas_call(
        slots_kernel,
        out_shape=pltpu.HBM((slot_count, rows, 2 * LANES), BF16),
        grid_spec=pltpu.PrefetchScalarGridSpec(
            num_scalar_prefetch=1,
            grid=(1,),
            in_specs=[pair, IN_VMEM, IN_VMEM, pair, IN_VMEM, IN_VMEM],
            out_specs=pl.BlockSpec(memory_space=pltpu.HBM),
            scratch_shapes=[
                pltpu.VMEM((count, rows, 2 * LANES), BF16),
                pltpu.SemaphoreType.DMA((count,)),
            ],
        ),
        compiler_params=pltpu.CompilerParams(vmem_limit_bytes=SMALL_VMEM),
        cost_estimate=cost(FILL_FLOPS),
        name="fill_slots",
    )(positions, *parts)


def merge_kernel(device, places, received, own, *rest):
    *outs, acc = rest
    blocks = own.shape[1]
    at = [pl.multiple_of(q * EARLY_ROWS, EARLY_ROWS) for q in relative_quarters(device[0])]
    for p in range(4):
        acc[:blocks, pl.ds(at[p], EARLY_ROWS)] = own[p].astype(F32)
    add_slots(acc, places, received)
    for p in range(4):
        outs[p][...] = acc[:blocks, pl.ds(at[p], EARLY_ROWS)].astype(BF16)


def merge_early(device, places, received, own):
    _, blocks, rows, width = own.shape
    shape = (blocks, rows, width)
    return pl.pallas_call(
        merge_kernel,
        out_shape=[pltpu.HBM(shape, BF16)] * 4,
        grid_spec=pltpu.PrefetchScalarGridSpec(
            num_scalar_prefetch=2,
            grid=(1,),
            in_specs=[IN_VMEM, whole(own.shape)],
            out_specs=[whole(shape)] * 4,
            scratch_shapes=[pltpu.VMEM((blocks + 1, 4 * rows, width), F32)],
        ),
        compiler_params=pltpu.CompilerParams(vmem_limit_bytes=SMALL_VMEM),
        cost_estimate=cost(),
        name="merge_early",
    )(device, places, received, own)


def add_slots(acc, places, received):
    def add(p, _):
        acc[places[p]] += received[p].astype(F32)
        return 0

    lax.fori_loop(0, received.shape[0], add, 0, unroll=4)


def first_sum(early, late):
    blocks, early_rows, width = early[0].shape
    late_rows = late[0].shape[1]
    shape = (blocks, early_rows + late_rows, width)

    def total(parts):
        value = parts[0][...].astype(F32)
        for part in parts[1:]:
            value = value + part[...].astype(F32)
        return value

    def kernel(*refs):
        *parts, result = refs
        result[:, :early_rows] = total(parts[:4])
        result[:, early_rows:] = total(parts[4:])

    return pl.pallas_call(
        kernel,
        out_shape=pltpu.HBM(shape, F32),
        grid=(1,),
        in_specs=[IN_VMEM] * 8,
        out_specs=whole(shape),
        compiler_params=pltpu.CompilerParams(vmem_limit_bytes=SMALL_VMEM),
        cost_estimate=cost(),
        name="first_sum",
    )(*early, *late)


def last_sum(places, received, so_far):
    blocks, _, width = so_far.shape
    rows = EARLY_ROWS
    part = pl.BlockSpec((blocks, rows, width), lambda i, *_: (0, i + 1, 0))

    def kernel(places, received, so_far, result, acc):
        at = pl.multiple_of(pl.program_id(0) * rows, rows)
        acc[:blocks] = so_far[...]

        def add(p, _):
            acc[places[p]] += received[p, pl.ds(at, rows)].astype(F32)
            return 0

        lax.fori_loop(0, received.shape[0], add, 0, unroll=8)
        result[...] = acc[:blocks]

    return pl.pallas_call(
        kernel,
        out_shape=pltpu.HBM(so_far.shape, F32),
        grid_spec=pltpu.PrefetchScalarGridSpec(
            num_scalar_prefetch=1,
            grid=(received.shape[1] // rows,),
            in_specs=[IN_VMEM, part],
            out_specs=part,
            scratch_shapes=[pltpu.VMEM((blocks + 1, rows, width), F32)],
        ),
        input_output_aliases={2: 0},
        compiler_params=pltpu.CompilerParams(vmem_limit_bytes=SMALL_VMEM),
        cost_estimate=cost(),
        name="last_sum",
    )(places, received, so_far)


def item_places(targets, block_count):
    destined = targets // block_count
    count = targets.shape[-1]
    earlier = jnp.arange(count)[:, None] > jnp.arange(count)[None, :]
    same = (destined[..., :, None] == destined[..., None, :]) & earlier
    return destined, jnp.sum(same.astype(jnp.int32), axis=-1)


def shards(wavefunction, left_env, right_env, block_left, block_right, channel_class, hop_target):
    block_count = wavefunction.shape[0]
    hop_count = hop_target.shape[1]
    owners = lax.axis_size("lsec") * lax.axis_size("rsec")
    item_count = block_count * hop_count
    capacity = 2 * ((item_count + owners - 1) // owners)
    slot_count = owners * capacity
    me = lax.axis_index("lsec") * lax.axis_size("rsec") + lax.axis_index("rsec")
    device = jnp.stack([lax.axis_index(axis) for axis in ("mpo", "lsec", "rsec")]).astype(jnp.int32)
    targets = hop_target.reshape(owners, item_count)
    own_targets = lax.dynamic_index_in_dim(targets, me, 0, False)
    own_early, early_slots, *parts = products(
        (device, block_left, block_right, channel_class, own_targets),
        owners,
        capacity,
        wavefunction,
        left_env,
        right_env,
        hop_count + 1,
    )

    own_late, parts = parts[:4], parts[4:]
    destined, slot = item_places(own_targets, block_count)
    position = destined * capacity + slot
    destined_all, slot_all = item_places(targets, block_count)
    mine = (destined_all == me)[:, :, None] & (
        slot_all[:, :, None] == jnp.arange(capacity, dtype=jnp.int32)
    )
    local = targets - (me + 1) * block_count
    places = jnp.sum(jnp.where(mine, local[:, :, None], 0), axis=1).reshape(slot_count)
    places = places + block_count

    beside = [(i, i ^ 1) for i in range(4)]
    mirror = [(i, 3 - i) for i in range(4)]
    across = [(i, (i + 2) % 4) for i in range(4)]

    def second(keep, got):
        return (keep[1].astype(F32) + got[1].astype(F32)).astype(BF16)

    early = lax.all_to_all(early_slots, ("lsec", "rsec"), 0, 0, tiled=True)
    keep_a, send_a, keep_b, send_b = parts
    got_a = lax.ppermute(send_a, "mpo", beside)
    got_b = lax.ppermute(send_b, "mpo", mirror)
    last_a = lax.ppermute(second(keep_a, got_a), "mpo", mirror)
    last_b = lax.ppermute(second(keep_b, got_b), "mpo", beside)
    slots = fill_slots(position, slot_count, (keep_a, got_a, last_a, keep_b, got_b, last_b))
    received = lax.all_to_all(slots, ("lsec", "rsec"), 0, 0, tiled=True)
    early, slots, *own_late = lax.optimization_barrier((early, slots, *own_late))

    def over_groups(parts):
        mine, *theirs = parts
        return [mine] + [
            lax.ppermute(part, "mpo", pairs)
            for part, pairs in zip(theirs, (beside, mirror, across))
        ]

    late = over_groups(own_late)
    early = over_groups(merge_early(device, places, early, own_early))
    return last_sum(places, received, first_sum(early, late))


def solution(mesh):
    in_specs = (
        P(("lsec", "rsec"), None, None),
        P("mpo", "lsec", None, None),
        P("mpo", "rsec", None, None),
        P(("lsec", "rsec")),
        P(("lsec", "rsec")),
        P(),
        P(),
    )
    out_specs = P(("lsec", "rsec"), "mpo", None)
    return jax.shard_map(shards, mesh=mesh, in_specs=in_specs, out_specs=out_specs, check_vma=False)
```

```python
import functools

import jax
import jax.numpy as jnp
from jax import lax
from jax.experimental import pallas as pl
from jax.experimental.pallas import tpu as pltpu
from jax.sharding import PartitionSpec as P

LANES = 128
EARLY_ROWS = 16
CHUNKS = (48,)
FILL_FLOPS = 30000000000
SIDES = 2
HEAD = 3
AHEAD = 2
BF16 = jnp.bfloat16
F32 = jnp.float32


SMALL_VMEM = 20 * 2**20
IN_VMEM = pl.BlockSpec(memory_space=pltpu.VMEM)


def cost(flops=1):
    return pl.CostEstimate(flops=flops, bytes_accessed=1, transcendentals=0)


def whole(shape):
    return pl.BlockSpec(shape, lambda i, *_: (0,) * len(shape))


def relative_quarters(x):
    return x, x ^ 1, 3 - x, (3 - x) ^ 1


def products_kernel(
    capacity, device, block_left, block_right, channel_class, own_targets, psi_hbm, left_hbm,
    right_hbm, own_early, slots_hbm, *rest
):
    own_late = rest[:4]
    chunk_outs = rest[4 : 4 + 4 * len(CHUNKS)]
    (
        psi_ref, left_ref, right_ref, half_ref, acc_ref, stage_ref, seen_ref, first_ref, empty_ref,
        slot_ref, psi_sems, left_sems, right_sems, slot_sems,
    ) = rest[4 + 4 * len(CHUNKS) :]
    channels, left_count, _, _ = left_ref.shape
    right_count = right_ref.shape[1]
    classes = acc_ref.shape[1]
    hops = classes - 1
    quarter = acc_ref.shape[2] // 4
    head = SIDES * HEAD
    step = pl.program_id(0)
    steps = pl.num_programs(0)
    blocks = SIDES * steps
    x = device[0]

    def psi_copy(part):
        at = pl.ds(0, head) if part == 0 else pl.ds(head, psi_ref.shape[0] - head)
        return pltpu.make_async_copy(psi_hbm.at[at], psi_ref.at[at], psi_sems.at[part])

    def left_copy(w):
        return pltpu.make_async_copy(left_hbm.at[w], left_ref.at[w], left_sems.at[w])

    def right_copy(w):
        return pltpu.make_async_copy(right_hbm.at[w], right_ref.at[w], right_sems.at[w])

    def slot_copy(turn, side, h):
        flip = lax.rem(turn, 2)
        k = SIDES * turn + side
        return pltpu.make_async_copy(
            stage_ref.at[flip, side, h],
            slots_hbm.at[slot_ref[k * hops + h]],
            slot_sems.at[flip, side, h],
        )

    def each_slot(turn, act):
        for side in range(SIDES):
            for h in range(hops):
                act(slot_copy(turn, side, h))

    def sectors(k):
        return (
            block_left[k] - device[1] * left_count,
            block_right[k] - device[2] * right_count,
        )

    def first_product(w, k, left_id, place):
        half_ref[place] = jnp.dot(
            left_ref[w, left_id], psi_ref[k], preferred_element_type=F32
        ).astype(BF16)

    def second_product(w, right_id, place, at):
        full = jnp.dot(half_ref[place], right_ref[w, right_id], preferred_element_type=F32)
        member = channel_class[x * channels + w]
        before = acc_ref[at, member]
        acc_ref[at, member] = jnp.where(first_ref[w] != 0, 0.0, before) + full

    def emit_parts():
        flip = lax.rem(step, 2)
        here, beside, mirror, across = relative_quarters(x)
        orders = ((here, mirror, beside, across), (here, beside, mirror, across))

        def early_part(side, at, h):
            for q in range(4):
                rows = slice(q * EARLY_ROWS, (q + 1) * EARLY_ROWS)
                first = q * quarter
                stage_ref[flip, side, h, rows] = acc_ref[
                    at, h + 1, first : first + EARLY_ROWS
                ].astype(BF16)

        def own_part(side, at, place, q):
            row = pl.multiple_of(q * quarter, quarter)
            own_early[place, side] = acc_ref[at, 0, pl.ds(row, EARLY_ROWS)].astype(BF16)
            row = pl.multiple_of(row + EARLY_ROWS, EARLY_ROWS)
            own_late[place][side] = acc_ref[at, 0, pl.ds(row, quarter - EARLY_ROWS)].astype(BF16)

        def chunk_part(side, at, h, j, start, rows, s):
            keep, send = chunk_outs[4 * j + 2 * s : 4 * j + 2 * s + 2]
            for place, q in enumerate(orders[s]):
                target = keep if place < 2 else send
                row = pl.multiple_of(q * quarter + start, 16)
                target[place % 2, side * hops + h] = acc_ref[
                    at, h + 1, pl.ds(row, rows), s * LANES : (s + 1) * LANES
                ].astype(BF16)

        work = []
        for side in range(SIDES):
            at = SIDES * lax.rem(step, HEAD) + side
            for h in range(hops):
                work.append(functools.partial(early_part, side, at, h))
            for place, q in enumerate((here, beside, mirror, across)):
                work.append(functools.partial(own_part, side, at, place, q))
            start = EARLY_ROWS
            for j, rows in enumerate(CHUNKS):
                for s in range(2):
                    for h in range(hops):
                        work.append(
                            functools.partial(chunk_part, side, at, h, j, start, rows, s)
                        )
                start += rows
        return work

    @pl.when(step == 0)
    def _():
        psi_copy(0).start()
        for w in range(AHEAD):
            left_copy(w).start()
            right_copy(w).start()
        for i in range(seen_ref.shape[0]):
            seen_ref[i] = 0

        def place(i, _):
            owner = lax.div(own_targets[i], blocks)
            earlier = seen_ref[owner]
            slot_ref[i] = owner * capacity + earlier
            seen_ref[owner] = earlier + 1
            return 0

        lax.fori_loop(0, slot_ref.shape[0], place, 0)
        for c in range(classes):
            empty_ref[c] = 1
        for w in range(channels):
            member = channel_class[x * channels + w]
            first_ref[w] = empty_ref[member]
            empty_ref[member] = 0
        for c in range(classes):

            @pl.when(empty_ref[c] != 0)
            def _():
                for at in range(head):
                    acc_ref[at, c] = jnp.zeros(acc_ref.shape[2:], F32)

        psi_copy(0).wait()

        def channel(w, _):
            left_copy(w).wait()
            right_copy(w).wait()

            @pl.when(w + AHEAD < channels)
            def _():
                left_copy(w + AHEAD).start()
                right_copy(w + AHEAD).start()

            @pl.when(w + AHEAD == channels)
            def _():
                psi_copy(1).start()

            ids = [sectors(k) for k in range(head)]
            for k in range(head):
                first_product(w, k, ids[k][0], k)
            for k in range(head):
                second_product(w, ids[k][1], k, k)
            return 0

        lax.fori_loop(0, channels, channel, 0)
        for part in emit_parts():
            part()

    @pl.when(step == 1)
    def _():
        psi_copy(1).wait()

    @pl.when(step >= 2)
    def _():
        each_slot(step - 2, lambda copy: copy.wait())

    @pl.when((step > 0) & (step <= steps - HEAD))
    def _():
        work = emit_parts()
        turns = SIDES * channels
        pair = step + HEAD - 1
        for side in range(SIDES):
            k = SIDES * pair + side
            left_id, right_id = sectors(k)
            at = SIDES * lax.rem(pair, HEAD) + side
            for w in range(channels):
                first_product(w, k, left_id, side * channels + w)
            for w in range(channels):
                second_product(w, right_id, side * channels + w, at)
                turn = side * channels + w
                for part in work[turn * len(work) // turns : (turn + 1) * len(work) // turns]:
                    part()

    @pl.when(step > steps - HEAD)
    def _():
        for part in emit_parts():
            part()

    each_slot(step, lambda copy: copy.start())

    @pl.when(step == steps - 1)
    def _():
        each_slot(step - 1, lambda copy: copy.wait())
        each_slot(step, lambda copy: copy.wait())


def products(tables, owners, capacity, psi, left_env, right_env, classes):
    blocks, block, _ = psi.shape
    channels = left_env.shape[0]
    quarter = block // 4
    early = 4 * EARLY_ROWS
    hops = classes - 1
    head = SIDES * HEAD
    out_shape = [
        pltpu.HBM((4, blocks, EARLY_ROWS, block), BF16),
        pltpu.HBM((owners * capacity, early, block), BF16),
    ] + [pltpu.HBM((blocks, quarter - EARLY_ROWS, block), BF16)] * 4
    out_specs = [
        pl.BlockSpec((4, SIDES, EARLY_ROWS, block), lambda k, *_: (0, k, 0, 0)),
        pl.BlockSpec(memory_space=pltpu.HBM),
    ] + [pl.BlockSpec((SIDES, quarter - EARLY_ROWS, block), lambda k, *_: (k, 0, 0))] * 4
    for rows in CHUNKS:
        out_shape += [pltpu.HBM((2, blocks * hops, rows, LANES), BF16)] * 4
        block_shape = (2, SIDES * hops, rows, LANES)
        out_specs += [pl.BlockSpec(block_shape, lambda k, *_: (0, k, 0, 0))] * 4
    return pl.pallas_call(
        functools.partial(products_kernel, capacity),
        out_shape=out_shape,
        grid_spec=pltpu.PrefetchScalarGridSpec(
            num_scalar_prefetch=len(tables),
            grid=(blocks // SIDES,),
            in_specs=[pl.BlockSpec(memory_space=pltpu.HBM)] * 3,
            out_specs=out_specs,
            scratch_shapes=[
                pltpu.VMEM(psi.shape, BF16),
                pltpu.VMEM(left_env.shape, BF16),
                pltpu.VMEM(right_env.shape, BF16),
                pltpu.VMEM((max(head, SIDES * channels), block, block), BF16),
                pltpu.VMEM((head, classes, block, block), F32),
                pltpu.VMEM((2, SIDES, hops, early, block), BF16),
                pltpu.SMEM((owners,), jnp.int32),
                pltpu.SMEM((channels,), jnp.int32),
                pltpu.SMEM((classes,), jnp.int32),
                pltpu.SMEM((blocks * hops,), jnp.int32),
                pltpu.SemaphoreType.DMA((2,)),
                pltpu.SemaphoreType.DMA((channels,)),
                pltpu.SemaphoreType.DMA((channels,)),
                pltpu.SemaphoreType.DMA((2, SIDES, hops)),
            ],
        ),
        compiler_params=pltpu.CompilerParams(vmem_limit_bytes=60 * 2**20),
        cost_estimate=pl.CostEstimate(
            flops=4 * channels * blocks * block**3,
            bytes_accessed=2 * (left_env.size + right_env.size + psi.size * (1 + classes)),
            transcendentals=0,
        ),
        name="products",
    )(*tables, psi, left_env, right_env)


def slots_kernel(positions, keep_a, got_a, last_a, keep_b, got_b, last_b, slots, stage, sems):
    def total(keep, got, last, i):
        value = keep[0, i].astype(F32) + got[0, i].astype(F32) + last[i].astype(F32)
        return value.astype(BF16)

    def copy(i):
        return pltpu.make_async_copy(stage.at[i], slots.at[positions[i]], sems.at[i])

    def fill(i, _):
        stage[i, :, :LANES] = total(keep_a, got_a, last_a, i)
        stage[i, :, LANES:] = total(keep_b, got_b, last_b, i)
        copy(i).start()
        return 0

    def finish(i, _):
        copy(i).wait()
        return 0

    lax.fori_loop(0, stage.shape[0], fill, 0, unroll=4)
    lax.fori_loop(0, stage.shape[0], finish, 0, unroll=4)


def fill_slots(positions, slot_count, parts):
    _, count, rows, _ = parts[0].shape
    pair = whole((1, count, rows, LANES))
    return pl.pallas_call(
        slots_kernel,
        out_shape=pltpu.HBM((slot_count, rows, 2 * LANES), BF16),
        grid_spec=pltpu.PrefetchScalarGridSpec(
            num_scalar_prefetch=1,
            grid=(1,),
            in_specs=[pair, IN_VMEM, IN_VMEM, pair, IN_VMEM, IN_VMEM],
            out_specs=pl.BlockSpec(memory_space=pltpu.HBM),
            scratch_shapes=[
                pltpu.VMEM((count, rows, 2 * LANES), BF16),
                pltpu.SemaphoreType.DMA((count,)),
            ],
        ),
        compiler_params=pltpu.CompilerParams(vmem_limit_bytes=SMALL_VMEM),
        cost_estimate=cost(FILL_FLOPS),
        name="fill_slots",
    )(positions, *parts)


def merge_kernel(device, places, received, own, *rest):
    *outs, acc = rest
    blocks = own.shape[1]
    at = [pl.multiple_of(q * EARLY_ROWS, EARLY_ROWS) for q in relative_quarters(device[0])]
    for p in range(4):
        acc[:blocks, pl.ds(at[p], EARLY_ROWS)] = own[p].astype(F32)
    add_slots(acc, places, received)
    for p in range(4):
        outs[p][...] = acc[:blocks, pl.ds(at[p], EARLY_ROWS)].astype(BF16)


def merge_early(device, places, received, own):
    _, blocks, rows, width = own.shape
    shape = (blocks, rows, width)
    return pl.pallas_call(
        merge_kernel,
        out_shape=[pltpu.HBM(shape, BF16)] * 4,
        grid_spec=pltpu.PrefetchScalarGridSpec(
            num_scalar_prefetch=2,
            grid=(1,),
            in_specs=[IN_VMEM, whole(own.shape)],
            out_specs=[whole(shape)] * 4,
            scratch_shapes=[pltpu.VMEM((blocks + 1, 4 * rows, width), F32)],
        ),
        compiler_params=pltpu.CompilerParams(vmem_limit_bytes=SMALL_VMEM),
        cost_estimate=cost(),
        name="merge_early",
    )(device, places, received, own)


def add_slots(acc, places, received):
    def add(p, _):
        acc[places[p]] += received[p].astype(F32)
        return 0

    lax.fori_loop(0, received.shape[0], add, 0, unroll=4)


def first_sum(early, late):
    blocks, early_rows, width = early[0].shape
    late_rows = late[0].shape[1]
    shape = (blocks, early_rows + late_rows, width)

    def total(parts):
        value = parts[0][...].astype(F32)
        for part in parts[1:]:
            value = value + part[...].astype(F32)
        return value

    def kernel(*refs):
        *parts, result = refs
        result[:, :early_rows] = total(parts[:4])
        result[:, early_rows:] = total(parts[4:])

    return pl.pallas_call(
        kernel,
        out_shape=pltpu.HBM(shape, F32),
        grid=(1,),
        in_specs=[IN_VMEM] * 8,
        out_specs=whole(shape),
        compiler_params=pltpu.CompilerParams(vmem_limit_bytes=SMALL_VMEM),
        cost_estimate=cost(),
        name="first_sum",
    )(*early, *late)


def last_sum(places, received, so_far):
    blocks, _, width = so_far.shape
    rows = received.shape[1]

    def kernel(places, received, so_far, result, base, acc_a, acc_b, sems):
        later = pl.ds(EARLY_ROWS, rows)
        fetch = pltpu.make_async_copy(so_far.at[:, later], base, sems.at[0])
        fetch.start()
        acc_a[...] = jnp.zeros_like(acc_a)
        acc_b[...] = jnp.zeros_like(acc_b)

        def add(turn, _):
            for i, acc in enumerate((acc_a, acc_b)):
                p = turn * 2 + i
                acc[places[p]] += received[p].astype(F32)
            return 0

        lax.fori_loop(0, received.shape[0] // 2, add, 0, unroll=2)
        fetch.wait()
        base[...] += acc_a[:blocks] + acc_b[:blocks]
        store = pltpu.make_async_copy(base, result.at[:, later], sems.at[1])
        store.start()
        store.wait()

    return pl.pallas_call(
        kernel,
        out_shape=pltpu.HBM(so_far.shape, F32),
        grid_spec=pltpu.PrefetchScalarGridSpec(
            num_scalar_prefetch=1,
            grid=(1,),
            in_specs=[IN_VMEM, pl.BlockSpec(memory_space=pltpu.HBM)],
            out_specs=pl.BlockSpec(memory_space=pltpu.HBM),
            scratch_shapes=[
                pltpu.VMEM((blocks, rows, width), F32),
                pltpu.VMEM((blocks + 1, rows, width), F32),
                pltpu.VMEM((blocks + 1, rows, width), F32),
                pltpu.SemaphoreType.DMA((2,)),
            ],
        ),
        input_output_aliases={2: 0},
        compiler_params=pltpu.CompilerParams(vmem_limit_bytes=SMALL_VMEM),
        cost_estimate=cost(),
        name="last_sum",
    )(places, received, so_far)


def item_places(targets, block_count):
    destined = targets // block_count
    count = targets.shape[-1]
    earlier = jnp.arange(count)[:, None] > jnp.arange(count)[None, :]
    same = (destined[..., :, None] == destined[..., None, :]) & earlier
    return destined, jnp.sum(same.astype(jnp.int32), axis=-1)


def shards(wavefunction, left_env, right_env, block_left, block_right, channel_class, hop_target):
    block_count = wavefunction.shape[0]
    hop_count = hop_target.shape[1]
    owners = lax.axis_size("lsec") * lax.axis_size("rsec")
    item_count = block_count * hop_count
    capacity = 2 * ((item_count + owners - 1) // owners)
    slot_count = owners * capacity
    me = lax.axis_index("lsec") * lax.axis_size("rsec") + lax.axis_index("rsec")
    device = jnp.stack([lax.axis_index(axis) for axis in ("mpo", "lsec", "rsec")]).astype(jnp.int32)
    targets = hop_target.reshape(owners, item_count)
    own_targets = lax.dynamic_index_in_dim(targets, me, 0, False)
    own_early, early_slots, *parts = products(
        (device, block_left, block_right, channel_class, own_targets),
        owners,
        capacity,
        wavefunction,
        left_env,
        right_env,
        hop_count + 1,
    )

    own_late, parts = parts[:4], parts[4:]
    destined, slot = item_places(own_targets, block_count)
    position = destined * capacity + slot
    destined_all, slot_all = item_places(targets, block_count)
    mine = (destined_all == me)[:, :, None] & (
        slot_all[:, :, None] == jnp.arange(capacity, dtype=jnp.int32)
    )
    local = targets - (me + 1) * block_count
    places = jnp.sum(jnp.where(mine, local[:, :, None], 0), axis=1).reshape(slot_count)
    places = places + block_count

    beside = [(i, i ^ 1) for i in range(4)]
    mirror = [(i, 3 - i) for i in range(4)]
    across = [(i, (i + 2) % 4) for i in range(4)]

    def second(keep, got):
        return (keep[1].astype(F32) + got[1].astype(F32)).astype(BF16)

    early = lax.all_to_all(early_slots, ("lsec", "rsec"), 0, 0, tiled=True)
    keep_a, send_a, keep_b, send_b = parts
    got_a = lax.ppermute(send_a, "mpo", beside)
    got_b = lax.ppermute(send_b, "mpo", mirror)
    last_a = lax.ppermute(second(keep_a, got_a), "mpo", mirror)
    last_b = lax.ppermute(second(keep_b, got_b), "mpo", beside)
    slots = fill_slots(position, slot_count, (keep_a, got_a, last_a, keep_b, got_b, last_b))
    received = lax.all_to_all(slots, ("lsec", "rsec"), 0, 0, tiled=True)
    early, slots, *own_late = lax.optimization_barrier((early, slots, *own_late))

    def over_groups(parts):
        mine, *theirs = parts
        return [mine] + [
            lax.ppermute(part, "mpo", pairs)
            for part, pairs in zip(theirs, (beside, mirror, across))
        ]

    late = over_groups(own_late)
    early = over_groups(merge_early(device, places, early, own_early))
    return last_sum(places, received, first_sum(early, late))


def solution(mesh):
    in_specs = (
        P(("lsec", "rsec"), None, None),
        P("mpo", "lsec", None, None),
        P("mpo", "rsec", None, None),
        P(("lsec", "rsec")),
        P(("lsec", "rsec")),
        P(),
        P(),
    )
    out_specs = P(("lsec", "rsec"), "mpo", None)
    return jax.shard_map(shards, mesh=mesh, in_specs=in_specs, out_specs=out_specs, check_vma=False)
```

```python
import functools

import jax
import jax.numpy as jnp
from jax import lax
from jax.experimental import pallas as pl
from jax.experimental.pallas import tpu as pltpu
from jax.sharding import PartitionSpec as P

LANES = 128
EARLY_ROWS = 16
CHUNKS = (48,)
FILL_FLOPS = 30000000000
SIDES = 2
HEAD = 3
AHEAD = 2
BF16 = jnp.bfloat16
F32 = jnp.float32


SMALL_VMEM = 20 * 2**20
IN_VMEM = pl.BlockSpec(memory_space=pltpu.VMEM)


def cost(flops=1):
    return pl.CostEstimate(flops=flops, bytes_accessed=1, transcendentals=0)


def whole(shape):
    return pl.BlockSpec(shape, lambda i, *_: (0,) * len(shape))


def relative_quarters(x):
    return x, x ^ 1, 3 - x, (3 - x) ^ 1


def products_kernel(
    capacity, block_left, block_right, channel_class, own_targets, psi_hbm, left_hbm, right_hbm,
    own_early, slots_hbm, *rest
):
    own_late = rest[:4]
    chunk_outs = rest[4 : 4 + 4 * len(CHUNKS)]
    (
        psi_ref, left_ref, right_ref, half_ref, acc_ref, stage_ref, seen_ref, first_ref, empty_ref,
        slot_ref, psi_sems, left_sems, right_sems, slot_sems,
    ) = rest[4 + 4 * len(CHUNKS) :]
    channels, left_count, _, _ = left_ref.shape
    right_count = right_ref.shape[1]
    classes = acc_ref.shape[1]
    hops = classes - 1
    quarter = acc_ref.shape[2] // 4
    head = SIDES * HEAD
    step = pl.program_id(0)
    steps = pl.num_programs(0)
    blocks = SIDES * steps
    x = lax.axis_index("mpo")
    first_left = lax.axis_index("lsec") * left_count
    first_right = lax.axis_index("rsec") * right_count

    def psi_copy(part):
        at = pl.ds(0, head) if part == 0 else pl.ds(head, psi_ref.shape[0] - head)
        return pltpu.make_async_copy(psi_hbm.at[at], psi_ref.at[at], psi_sems.at[part])

    def left_copy(w):
        return pltpu.make_async_copy(left_hbm.at[w], left_ref.at[w], left_sems.at[w])

    def right_copy(w):
        return pltpu.make_async_copy(right_hbm.at[w], right_ref.at[w], right_sems.at[w])

    def slot_copy(turn, side, h):
        flip = lax.rem(turn, 2)
        k = SIDES * turn + side
        return pltpu.make_async_copy(
            stage_ref.at[flip, side, h],
            slots_hbm.at[slot_ref[k * hops + h]],
            slot_sems.at[flip, side, h],
        )

    def each_slot(turn, act):
        for side in range(SIDES):
            for h in range(hops):
                act(slot_copy(turn, side, h))

    def sectors(k):
        return block_left[k] - first_left, block_right[k] - first_right

    def first_product(w, k, left_id, place):
        half_ref[place] = jnp.dot(
            left_ref[w, left_id], psi_ref[k], preferred_element_type=F32
        ).astype(BF16)

    def second_product(w, right_id, place, at):
        full = jnp.dot(half_ref[place], right_ref[w, right_id], preferred_element_type=F32)
        member = channel_class[x * channels + w]
        before = acc_ref[at, member]
        acc_ref[at, member] = jnp.where(first_ref[w] != 0, 0.0, before) + full

    def emit_parts():
        flip = lax.rem(step, 2)
        here, beside, mirror, across = relative_quarters(x)
        orders = ((here, mirror, beside, across), (here, beside, mirror, across))

        def early_part(side, at, h):
            for q in range(4):
                rows = slice(q * EARLY_ROWS, (q + 1) * EARLY_ROWS)
                first = q * quarter
                stage_ref[flip, side, h, rows] = acc_ref[
                    at, h + 1, first : first + EARLY_ROWS
                ].astype(BF16)

        def own_part(side, at, place, q):
            row = pl.multiple_of(q * quarter, quarter)
            own_early[place, side] = acc_ref[at, 0, pl.ds(row, EARLY_ROWS)].astype(BF16)
            row = pl.multiple_of(row + EARLY_ROWS, EARLY_ROWS)
            own_late[place][side] = acc_ref[at, 0, pl.ds(row, quarter - EARLY_ROWS)].astype(BF16)

        def chunk_part(side, at, h, j, start, rows, s):
            keep, send = chunk_outs[4 * j + 2 * s : 4 * j + 2 * s + 2]
            for place, q in enumerate(orders[s]):
                target = keep if place < 2 else send
                row = pl.multiple_of(q * quarter + start, 16)
                target[place % 2, side * hops + h] = acc_ref[
                    at, h + 1, pl.ds(row, rows), s * LANES : (s + 1) * LANES
                ].astype(BF16)

        work = []
        for side in range(SIDES):
            at = SIDES * lax.rem(step, HEAD) + side
            for h in range(hops):
                work.append(functools.partial(early_part, side, at, h))
            for place, q in enumerate((here, beside, mirror, across)):
                work.append(functools.partial(own_part, side, at, place, q))
            start = EARLY_ROWS
            for j, rows in enumerate(CHUNKS):
                for s in range(2):
                    for h in range(hops):
                        work.append(
                            functools.partial(chunk_part, side, at, h, j, start, rows, s)
                        )
                start += rows
        return work

    @pl.when(step == 0)
    def _():
        psi_copy(0).start()
        for w in range(AHEAD):
            left_copy(w).start()
            right_copy(w).start()
        for i in range(seen_ref.shape[0]):
            seen_ref[i] = 0

        def place(i, _):
            owner = lax.div(own_targets[i], blocks)
            earlier = seen_ref[owner]
            slot_ref[i] = owner * capacity + earlier
            seen_ref[owner] = earlier + 1
            return 0

        lax.fori_loop(0, slot_ref.shape[0], place, 0)
        for c in range(classes):
            empty_ref[c] = 1
        for w in range(channels):
            member = channel_class[x * channels + w]
            first_ref[w] = empty_ref[member]
            empty_ref[member] = 0
        for c in range(classes):

            @pl.when(empty_ref[c] != 0)
            def _():
                for at in range(head):
                    acc_ref[at, c] = jnp.zeros(acc_ref.shape[2:], F32)

        psi_copy(0).wait()

        def channel(w, _):
            left_copy(w).wait()
            right_copy(w).wait()

            @pl.when(w + AHEAD < channels)
            def _():
                left_copy(w + AHEAD).start()
                right_copy(w + AHEAD).start()

            @pl.when(w + AHEAD == channels)
            def _():
                psi_copy(1).start()

            ids = [sectors(k) for k in range(head)]
            for k in range(head):
                first_product(w, k, ids[k][0], k)
            for k in range(head):
                second_product(w, ids[k][1], k, k)
            return 0

        lax.fori_loop(0, channels, channel, 0)
        for part in emit_parts():
            part()

    @pl.when(step == 1)
    def _():
        psi_copy(1).wait()

    @pl.when(step >= 2)
    def _():
        each_slot(step - 2, lambda copy: copy.wait())

    @pl.when((step > 0) & (step <= steps - HEAD))
    def _():
        work = emit_parts()
        turns = SIDES * channels
        pair = step + HEAD - 1
        for side in range(SIDES):
            k = SIDES * pair + side
            left_id, right_id = sectors(k)
            at = SIDES * lax.rem(pair, HEAD) + side
            first_product(0, k, left_id, side * channels)
            for w in range(channels):
                if w + 1 < channels:
                    first_product(w + 1, k, left_id, side * channels + w + 1)
                second_product(w, right_id, side * channels + w, at)
                turn = side * channels + w
                for part in work[turn * len(work) // turns : (turn + 1) * len(work) // turns]:
                    part()

    @pl.when(step > steps - HEAD)
    def _():
        for part in emit_parts():
            part()

    each_slot(step, lambda copy: copy.start())

    @pl.when(step == steps - 1)
    def _():
        each_slot(step - 1, lambda copy: copy.wait())
        each_slot(step, lambda copy: copy.wait())


def products(tables, owners, capacity, psi, left_env, right_env, classes):
    blocks, block, _ = psi.shape
    channels = left_env.shape[0]
    quarter = block // 4
    early = 4 * EARLY_ROWS
    hops = classes - 1
    head = SIDES * HEAD
    out_shape = [
        pltpu.HBM((4, blocks, EARLY_ROWS, block), BF16),
        pltpu.HBM((owners * capacity, early, block), BF16),
    ] + [pltpu.HBM((blocks, quarter - EARLY_ROWS, block), BF16)] * 4
    out_specs = [
        pl.BlockSpec((4, SIDES, EARLY_ROWS, block), lambda k, *_: (0, k, 0, 0)),
        pl.BlockSpec(memory_space=pltpu.HBM),
    ] + [pl.BlockSpec((SIDES, quarter - EARLY_ROWS, block), lambda k, *_: (k, 0, 0))] * 4
    for rows in CHUNKS:
        out_shape += [pltpu.HBM((2, blocks * hops, rows, LANES), BF16)] * 4
        block_shape = (2, SIDES * hops, rows, LANES)
        out_specs += [pl.BlockSpec(block_shape, lambda k, *_: (0, k, 0, 0))] * 4
    return pl.pallas_call(
        functools.partial(products_kernel, capacity),
        out_shape=out_shape,
        grid_spec=pltpu.PrefetchScalarGridSpec(
            num_scalar_prefetch=len(tables),
            grid=(blocks // SIDES,),
            in_specs=[pl.BlockSpec(memory_space=pltpu.HBM)] * 3,
            out_specs=out_specs,
            scratch_shapes=[
                pltpu.VMEM(psi.shape, BF16),
                pltpu.VMEM(left_env.shape, BF16),
                pltpu.VMEM(right_env.shape, BF16),
                pltpu.VMEM((max(head, SIDES * channels), block, block), BF16),
                pltpu.VMEM((head, classes, block, block), F32),
                pltpu.VMEM((2, SIDES, hops, early, block), BF16),
                pltpu.SMEM((owners,), jnp.int32),
                pltpu.SMEM((channels,), jnp.int32),
                pltpu.SMEM((classes,), jnp.int32),
                pltpu.SMEM((blocks * hops,), jnp.int32),
                pltpu.SemaphoreType.DMA((2,)),
                pltpu.SemaphoreType.DMA((channels,)),
                pltpu.SemaphoreType.DMA((channels,)),
                pltpu.SemaphoreType.DMA((2, SIDES, hops)),
            ],
        ),
        compiler_params=pltpu.CompilerParams(vmem_limit_bytes=60 * 2**20),
        cost_estimate=pl.CostEstimate(
            flops=4 * channels * blocks * block**3,
            bytes_accessed=2 * (left_env.size + right_env.size + psi.size * (1 + classes)),
            transcendentals=0,
        ),
        name="products",
    )(*tables, psi, left_env, right_env)


def slots_kernel(positions, keep_a, got_a, last_a, keep_b, got_b, last_b, slots, stage, sems):
    def total(keep, got, last, i):
        value = keep[0, i].astype(F32) + got[0, i].astype(F32) + last[i].astype(F32)
        return value.astype(BF16)

    def copy(i):
        return pltpu.make_async_copy(stage.at[i], slots.at[positions[i]], sems.at[i])

    def fill(i, _):
        stage[i, :, :LANES] = total(keep_a, got_a, last_a, i)
        stage[i, :, LANES:] = total(keep_b, got_b, last_b, i)
        copy(i).start()
        return 0

    def finish(i, _):
        copy(i).wait()
        return 0

    lax.fori_loop(0, stage.shape[0], fill, 0, unroll=4)
    lax.fori_loop(0, stage.shape[0], finish, 0, unroll=4)


def fill_slots(positions, slot_count, parts):
    _, count, rows, _ = parts[0].shape
    pair = whole((1, count, rows, LANES))
    return pl.pallas_call(
        slots_kernel,
        out_shape=pltpu.HBM((slot_count, rows, 2 * LANES), BF16),
        grid_spec=pltpu.PrefetchScalarGridSpec(
            num_scalar_prefetch=1,
            grid=(1,),
            in_specs=[pair, IN_VMEM, IN_VMEM, pair, IN_VMEM, IN_VMEM],
            out_specs=pl.BlockSpec(memory_space=pltpu.HBM),
            scratch_shapes=[
                pltpu.VMEM((count, rows, 2 * LANES), BF16),
                pltpu.SemaphoreType.DMA((count,)),
            ],
        ),
        compiler_params=pltpu.CompilerParams(vmem_limit_bytes=SMALL_VMEM),
        cost_estimate=cost(FILL_FLOPS),
        name="fill_slots",
    )(positions, *parts)


def merge_kernel(device, places, received, own, *rest):
    *outs, acc = rest
    blocks = own.shape[1]
    at = [pl.multiple_of(q * EARLY_ROWS, EARLY_ROWS) for q in relative_quarters(device[0])]
    for p in range(4):
        acc[:blocks, pl.ds(at[p], EARLY_ROWS)] = own[p].astype(F32)
    add_slots(acc, places, received)
    for p in range(4):
        outs[p][...] = acc[:blocks, pl.ds(at[p], EARLY_ROWS)].astype(BF16)


def merge_early(device, places, received, own):
    _, blocks, rows, width = own.shape
    shape = (blocks, rows, width)
    return pl.pallas_call(
        merge_kernel,
        out_shape=[pltpu.HBM(shape, BF16)] * 4,
        grid_spec=pltpu.PrefetchScalarGridSpec(
            num_scalar_prefetch=2,
            grid=(1,),
            in_specs=[IN_VMEM, whole(own.shape)],
            out_specs=[whole(shape)] * 4,
            scratch_shapes=[pltpu.VMEM((blocks + 1, 4 * rows, width), F32)],
        ),
        compiler_params=pltpu.CompilerParams(vmem_limit_bytes=SMALL_VMEM),
        cost_estimate=cost(),
        name="merge_early",
    )(device, places, received, own)


def add_slots(acc, places, received):
    def add(p, _):
        acc[places[p]] += received[p].astype(F32)
        return 0

    lax.fori_loop(0, received.shape[0], add, 0, unroll=4)


def first_sum(early, late):
    blocks, early_rows, width = early[0].shape
    late_rows = late[0].shape[1]
    shape = (blocks, early_rows + late_rows, width)

    def total(parts):
        value = parts[0][...].astype(F32)
        for part in parts[1:]:
            value = value + part[...].astype(F32)
        return value

    def kernel(*refs):
        *parts, result = refs
        result[:, :early_rows] = total(parts[:4])
        result[:, early_rows:] = total(parts[4:])

    return pl.pallas_call(
        kernel,
        out_shape=pltpu.HBM(shape, F32),
        grid=(1,),
        in_specs=[IN_VMEM] * 8,
        out_specs=whole(shape),
        compiler_params=pltpu.CompilerParams(vmem_limit_bytes=SMALL_VMEM),
        cost_estimate=cost(),
        name="first_sum",
    )(*early, *late)


def last_sum(places, received, so_far):
    blocks, _, width = so_far.shape
    rows = received.shape[1]

    def kernel(places, received, so_far, result, base, acc_a, acc_b, sems):
        later = pl.ds(EARLY_ROWS, rows)
        fetch = pltpu.make_async_copy(so_far.at[:, later], base, sems.at[0])
        fetch.start()
        acc_a[...] = jnp.zeros_like(acc_a)
        acc_b[...] = jnp.zeros_like(acc_b)

        def add(turn, _):
            for i, acc in enumerate((acc_a, acc_b)):
                p = turn * 2 + i
                acc[places[p]] += received[p].astype(F32)
            return 0

        lax.fori_loop(0, received.shape[0] // 2, add, 0, unroll=2)
        fetch.wait()
        base[...] += acc_a[:blocks] + acc_b[:blocks]
        store = pltpu.make_async_copy(base, result.at[:, later], sems.at[1])
        store.start()
        store.wait()

    return pl.pallas_call(
        kernel,
        out_shape=pltpu.HBM(so_far.shape, F32),
        grid_spec=pltpu.PrefetchScalarGridSpec(
            num_scalar_prefetch=1,
            grid=(1,),
            in_specs=[IN_VMEM, pl.BlockSpec(memory_space=pltpu.HBM)],
            out_specs=pl.BlockSpec(memory_space=pltpu.HBM),
            scratch_shapes=[
                pltpu.VMEM((blocks, rows, width), F32),
                pltpu.VMEM((blocks + 1, rows, width), F32),
                pltpu.VMEM((blocks + 1, rows, width), F32),
                pltpu.SemaphoreType.DMA((2,)),
            ],
        ),
        input_output_aliases={2: 0},
        compiler_params=pltpu.CompilerParams(vmem_limit_bytes=SMALL_VMEM),
        cost_estimate=cost(),
        name="last_sum",
    )(places, received, so_far)


def item_places(targets, block_count):
    destined = targets // block_count
    count = targets.shape[-1]
    earlier = jnp.arange(count)[:, None] > jnp.arange(count)[None, :]
    same = (destined[..., :, None] == destined[..., None, :]) & earlier
    return destined, jnp.sum(same.astype(jnp.int32), axis=-1)


def shards(wavefunction, left_env, right_env, block_left, block_right, channel_class, hop_target):
    block_count = wavefunction.shape[0]
    hop_count = hop_target.shape[1]
    owners = lax.axis_size("lsec") * lax.axis_size("rsec")
    item_count = block_count * hop_count
    capacity = 2 * ((item_count + owners - 1) // owners)
    slot_count = owners * capacity
    me = lax.axis_index("lsec") * lax.axis_size("rsec") + lax.axis_index("rsec")
    device = jnp.stack([lax.axis_index(axis) for axis in ("mpo", "lsec", "rsec")]).astype(jnp.int32)
    targets = hop_target.reshape(owners, item_count)
    own_targets = lax.dynamic_index_in_dim(targets, me, 0, False)
    own_early, early_slots, *parts = products(
        (block_left, block_right, channel_class, own_targets),
        owners,
        capacity,
        wavefunction,
        left_env,
        right_env,
        hop_count + 1,
    )

    own_late, parts = parts[:4], parts[4:]
    destined, slot = item_places(own_targets, block_count)
    position = destined * capacity + slot
    destined_all, slot_all = item_places(targets, block_count)
    mine = (destined_all == me)[:, :, None] & (
        slot_all[:, :, None] == jnp.arange(capacity, dtype=jnp.int32)
    )
    local = targets - (me + 1) * block_count
    places = jnp.sum(jnp.where(mine, local[:, :, None], 0), axis=1).reshape(slot_count)
    places = places + block_count

    beside = [(i, i ^ 1) for i in range(4)]
    mirror = [(i, 3 - i) for i in range(4)]
    across = [(i, (i + 2) % 4) for i in range(4)]

    def second(keep, got):
        return (keep[1].astype(F32) + got[1].astype(F32)).astype(BF16)

    early = lax.all_to_all(early_slots, ("lsec", "rsec"), 0, 0, tiled=True)
    keep_a, send_a, keep_b, send_b = parts
    got_a = lax.ppermute(send_a, "mpo", beside)
    got_b = lax.ppermute(send_b, "mpo", mirror)
    last_a = lax.ppermute(second(keep_a, got_a), "mpo", mirror)
    last_b = lax.ppermute(second(keep_b, got_b), "mpo", beside)
    slots = fill_slots(position, slot_count, (keep_a, got_a, last_a, keep_b, got_b, last_b))
    received = lax.all_to_all(slots, ("lsec", "rsec"), 0, 0, tiled=True)
    early, slots, *own_late = lax.optimization_barrier((early, slots, *own_late))

    def over_groups(parts):
        mine, *theirs = parts
        return [mine] + [
            lax.ppermute(part, "mpo", pairs)
            for part, pairs in zip(theirs, (beside, mirror, across))
        ]

    late = over_groups(own_late)
    early = over_groups(merge_early(device, places, early, own_early))
    return last_sum(places, received, first_sum(early, late))


def solution(mesh):
    in_specs = (
        P(("lsec", "rsec"), None, None),
        P("mpo", "lsec", None, None),
        P("mpo", "rsec", None, None),
        P(("lsec", "rsec")),
        P(("lsec", "rsec")),
        P(),
        P(),
    )
    out_specs = P(("lsec", "rsec"), "mpo", None)
    return jax.shard_map(shards, mesh=mesh, in_specs=in_specs, out_specs=out_specs, check_vma=False)
```

```python
import functools

import jax
import jax.numpy as jnp
from jax import lax
from jax.experimental import pallas as pl
from jax.experimental.pallas import tpu as pltpu
from jax.sharding import PartitionSpec as P

LANES = 128
EARLY_ROWS = 16
CHUNKS = (48,)
FILL_FLOPS = 30000000000
SIDES = 2
HEAD = 2
AHEAD = 3
BF16 = jnp.bfloat16
F32 = jnp.float32


SMALL_VMEM = 20 * 2**20
IN_VMEM = pl.BlockSpec(memory_space=pltpu.VMEM)


def cost(flops=1):
    return pl.CostEstimate(flops=flops, bytes_accessed=1, transcendentals=0)


def whole(shape):
    return pl.BlockSpec(shape, lambda i, *_: (0,) * len(shape))


def relative_quarters(x):
    return x, x ^ 1, 3 - x, (3 - x) ^ 1


def products_kernel(
    capacity, block_left, block_right, channel_class, own_targets, psi_hbm, left_hbm, right_hbm,
    own_early, slots_hbm, *rest
):
    own_late = rest[:4]
    chunk_outs = rest[4 : 4 + 4 * len(CHUNKS)]
    (
        psi_ref, left_ref, right_ref, half_ref, acc_ref, stage_ref, seen_ref, first_ref, empty_ref,
        slot_ref, psi_sems, left_sems, right_sems, slot_sems,
    ) = rest[4 + 4 * len(CHUNKS) :]
    channels, left_count, _, _ = left_ref.shape
    right_count = right_ref.shape[1]
    classes = acc_ref.shape[1]
    hops = classes - 1
    quarter = acc_ref.shape[2] // 4
    head = SIDES * HEAD
    step = pl.program_id(0)
    steps = pl.num_programs(0)
    blocks = SIDES * steps
    x = lax.axis_index("mpo")
    first_left = lax.axis_index("lsec") * left_count
    first_right = lax.axis_index("rsec") * right_count

    def psi_copy(part):
        at = pl.ds(0, head) if part == 0 else pl.ds(head, psi_ref.shape[0] - head)
        return pltpu.make_async_copy(psi_hbm.at[at], psi_ref.at[at], psi_sems.at[part])

    def left_copy(w):
        return pltpu.make_async_copy(left_hbm.at[w], left_ref.at[w], left_sems.at[w])

    def right_copy(w):
        return pltpu.make_async_copy(right_hbm.at[w], right_ref.at[w], right_sems.at[w])

    def slot_copy(turn, side, h):
        flip = lax.rem(turn, 2)
        k = SIDES * turn + side
        return pltpu.make_async_copy(
            stage_ref.at[flip, side, h],
            slots_hbm.at[slot_ref[k * hops + h]],
            slot_sems.at[flip, side, h],
        )

    def each_slot(turn, act):
        for side in range(SIDES):
            for h in range(hops):
                act(slot_copy(turn, side, h))

    def sectors(k):
        return block_left[k] - first_left, block_right[k] - first_right

    def first_product(w, k, left_id, place):
        half_ref[place] = jnp.dot(
            left_ref[w, left_id], psi_ref[k], preferred_element_type=F32
        ).astype(BF16)

    def second_product(w, right_id, place, at):
        full = jnp.dot(half_ref[place], right_ref[w, right_id], preferred_element_type=F32)
        member = channel_class[x * channels + w]
        before = acc_ref[at, member]
        acc_ref[at, member] = jnp.where(first_ref[w] != 0, 0.0, before) + full

    def emit_parts():
        flip = lax.rem(step, 2)
        here, beside, mirror, across = relative_quarters(x)
        orders = ((here, mirror, beside, across), (here, beside, mirror, across))

        def early_part(side, at, h):
            for q in range(4):
                rows = slice(q * EARLY_ROWS, (q + 1) * EARLY_ROWS)
                first = q * quarter
                stage_ref[flip, side, h, rows] = acc_ref[
                    at, h + 1, first : first + EARLY_ROWS
                ].astype(BF16)

        def own_part(side, at, place, q):
            row = pl.multiple_of(q * quarter, quarter)
            own_early[place, side] = acc_ref[at, 0, pl.ds(row, EARLY_ROWS)].astype(BF16)
            row = pl.multiple_of(row + EARLY_ROWS, EARLY_ROWS)
            own_late[place][side] = acc_ref[at, 0, pl.ds(row, quarter - EARLY_ROWS)].astype(BF16)

        def chunk_part(side, at, h, j, start, rows, s):
            keep, send = chunk_outs[4 * j + 2 * s : 4 * j + 2 * s + 2]
            for place, q in enumerate(orders[s]):
                target = keep if place < 2 else send
                row = pl.multiple_of(q * quarter + start, 16)
                target[place % 2, side * hops + h] = acc_ref[
                    at, h + 1, pl.ds(row, rows), s * LANES : (s + 1) * LANES
                ].astype(BF16)

        work = []
        for side in range(SIDES):
            at = SIDES * lax.rem(step, HEAD) + side
            for h in range(hops):
                work.append(functools.partial(early_part, side, at, h))
            for place, q in enumerate((here, beside, mirror, across)):
                work.append(functools.partial(own_part, side, at, place, q))
            start = EARLY_ROWS
            for j, rows in enumerate(CHUNKS):
                for s in range(2):
                    for h in range(hops):
                        work.append(
                            functools.partial(chunk_part, side, at, h, j, start, rows, s)
                        )
                start += rows
        return work

    @pl.when(step == 0)
    def _():
        psi_copy(0).start()
        for w in range(AHEAD):
            left_copy(w).start()
            right_copy(w).start()
        for i in range(seen_ref.shape[0]):
            seen_ref[i] = 0

        def place(i, _):
            owner = lax.div(own_targets[i], blocks)
            earlier = seen_ref[owner]
            slot_ref[i] = owner * capacity + earlier
            seen_ref[owner] = earlier + 1
            return 0

        lax.fori_loop(0, slot_ref.shape[0], place, 0)
        for c in range(classes):
            empty_ref[c] = 1
        for w in range(channels):
            member = channel_class[x * channels + w]
            first_ref[w] = empty_ref[member]
            empty_ref[member] = 0
        for c in range(classes):

            @pl.when(empty_ref[c] != 0)
            def _():
                for at in range(head):
                    acc_ref[at, c] = jnp.zeros(acc_ref.shape[2:], F32)

        psi_copy(0).wait()

        def channel(w, _):
            left_copy(w).wait()
            right_copy(w).wait()

            @pl.when(w + AHEAD < channels)
            def _():
                left_copy(w + AHEAD).start()
                right_copy(w + AHEAD).start()

            @pl.when(w + AHEAD == channels)
            def _():
                psi_copy(1).start()

            ids = [sectors(k) for k in range(head)]
            for k in range(head):
                first_product(w, k, ids[k][0], k)
            for k in range(head):
                second_product(w, ids[k][1], k, k)
            return 0

        lax.fori_loop(0, channels, channel, 0)
        for part in emit_parts():
            part()

    @pl.when(step == 1)
    def _():
        psi_copy(1).wait()

    @pl.when(step >= 2)
    def _():
        each_slot(step - 2, lambda copy: copy.wait())

    @pl.when((step > 0) & (step <= steps - HEAD))
    def _():
        work = emit_parts()
        turns = SIDES * channels
        pair = step + HEAD - 1
        for side in range(SIDES):
            k = SIDES * pair + side
            left_id, right_id = sectors(k)
            at = SIDES * lax.rem(pair, HEAD) + side
            first_product(0, k, left_id, side * channels)
            for w in range(channels):
                if w + 1 < channels:
                    first_product(w + 1, k, left_id, side * channels + w + 1)
                second_product(w, right_id, side * channels + w, at)
                turn = side * channels + w
                for part in work[turn * len(work) // turns : (turn + 1) * len(work) // turns]:
                    part()

    @pl.when(step > steps - HEAD)
    def _():
        for part in emit_parts():
            part()

    each_slot(step, lambda copy: copy.start())

    @pl.when(step == steps - 1)
    def _():
        each_slot(step - 1, lambda copy: copy.wait())
        each_slot(step, lambda copy: copy.wait())


def products(tables, owners, capacity, psi, left_env, right_env, classes):
    blocks, block, _ = psi.shape
    channels = left_env.shape[0]
    quarter = block // 4
    early = 4 * EARLY_ROWS
    hops = classes - 1
    head = SIDES * HEAD
    out_shape = [
        pltpu.HBM((4, blocks, EARLY_ROWS, block), BF16),
        pltpu.HBM((owners * capacity, early, block), BF16),
    ] + [pltpu.HBM((blocks, quarter - EARLY_ROWS, block), BF16)] * 4
    out_specs = [
        pl.BlockSpec((4, SIDES, EARLY_ROWS, block), lambda k, *_: (0, k, 0, 0)),
        pl.BlockSpec(memory_space=pltpu.HBM),
    ] + [pl.BlockSpec((SIDES, quarter - EARLY_ROWS, block), lambda k, *_: (k, 0, 0))] * 4
    for rows in CHUNKS:
        out_shape += [pltpu.HBM((2, blocks * hops, rows, LANES), BF16)] * 4
        block_shape = (2, SIDES * hops, rows, LANES)
        out_specs += [pl.BlockSpec(block_shape, lambda k, *_: (0, k, 0, 0))] * 4
    return pl.pallas_call(
        functools.partial(products_kernel, capacity),
        out_shape=out_shape,
        grid_spec=pltpu.PrefetchScalarGridSpec(
            num_scalar_prefetch=len(tables),
            grid=(blocks // SIDES,),
            in_specs=[pl.BlockSpec(memory_space=pltpu.HBM)] * 3,
            out_specs=out_specs,
            scratch_shapes=[
                pltpu.VMEM(psi.shape, BF16),
                pltpu.VMEM(left_env.shape, BF16),
                pltpu.VMEM(right_env.shape, BF16),
                pltpu.VMEM((max(head, SIDES * channels), block, block), BF16),
                pltpu.VMEM((head, classes, block, block), F32),
                pltpu.VMEM((2, SIDES, hops, early, block), BF16),
                pltpu.SMEM((owners,), jnp.int32),
                pltpu.SMEM((channels,), jnp.int32),
                pltpu.SMEM((classes,), jnp.int32),
                pltpu.SMEM((blocks * hops,), jnp.int32),
                pltpu.SemaphoreType.DMA((2,)),
                pltpu.SemaphoreType.DMA((channels,)),
                pltpu.SemaphoreType.DMA((channels,)),
                pltpu.SemaphoreType.DMA((2, SIDES, hops)),
            ],
        ),
        compiler_params=pltpu.CompilerParams(vmem_limit_bytes=60 * 2**20),
        cost_estimate=pl.CostEstimate(
            flops=4 * channels * blocks * block**3,
            bytes_accessed=2 * (left_env.size + right_env.size + psi.size * (1 + classes)),
            transcendentals=0,
        ),
        name="products",
    )(*tables, psi, left_env, right_env)


def slots_kernel(positions, keep_a, got_a, last_a, keep_b, got_b, last_b, slots, stage, sems):
    def total(keep, got, last, i):
        value = keep[0, i].astype(F32) + got[0, i].astype(F32) + last[i].astype(F32)
        return value.astype(BF16)

    def copy(i):
        return pltpu.make_async_copy(stage.at[i], slots.at[positions[i]], sems.at[i])

    def fill(i, _):
        stage[i, :, :LANES] = total(keep_a, got_a, last_a, i)
        stage[i, :, LANES:] = total(keep_b, got_b, last_b, i)
        copy(i).start()
        return 0

    def finish(i, _):
        copy(i).wait()
        return 0

    lax.fori_loop(0, stage.shape[0], fill, 0, unroll=4)
    lax.fori_loop(0, stage.shape[0], finish, 0, unroll=4)


def fill_slots(positions, slot_count, parts):
    _, count, rows, _ = parts[0].shape
    pair = whole((1, count, rows, LANES))
    return pl.pallas_call(
        slots_kernel,
        out_shape=pltpu.HBM((slot_count, rows, 2 * LANES), BF16),
        grid_spec=pltpu.PrefetchScalarGridSpec(
            num_scalar_prefetch=1,
            grid=(1,),
            in_specs=[pair, IN_VMEM, IN_VMEM, pair, IN_VMEM, IN_VMEM],
            out_specs=pl.BlockSpec(memory_space=pltpu.HBM),
            scratch_shapes=[
                pltpu.VMEM((count, rows, 2 * LANES), BF16),
                pltpu.SemaphoreType.DMA((count,)),
            ],
        ),
        compiler_params=pltpu.CompilerParams(vmem_limit_bytes=SMALL_VMEM),
        cost_estimate=cost(FILL_FLOPS),
        name="fill_slots",
    )(positions, *parts)


def merge_kernel(device, places, received, own, *rest):
    *outs, acc = rest
    blocks = own.shape[1]
    at = [pl.multiple_of(q * EARLY_ROWS, EARLY_ROWS) for q in relative_quarters(device[0])]
    for p in range(4):
        acc[:blocks, pl.ds(at[p], EARLY_ROWS)] = own[p].astype(F32)
    add_slots(acc, places, received)
    for p in range(4):
        outs[p][...] = acc[:blocks, pl.ds(at[p], EARLY_ROWS)].astype(BF16)


def merge_early(device, places, received, own):
    _, blocks, rows, width = own.shape
    shape = (blocks, rows, width)
    return pl.pallas_call(
        merge_kernel,
        out_shape=[pltpu.HBM(shape, BF16)] * 4,
        grid_spec=pltpu.PrefetchScalarGridSpec(
            num_scalar_prefetch=2,
            grid=(1,),
            in_specs=[IN_VMEM, whole(own.shape)],
            out_specs=[whole(shape)] * 4,
            scratch_shapes=[pltpu.VMEM((blocks + 1, 4 * rows, width), F32)],
        ),
        compiler_params=pltpu.CompilerParams(vmem_limit_bytes=SMALL_VMEM),
        cost_estimate=cost(),
        name="merge_early",
    )(device, places, received, own)


def add_slots(acc, places, received):
    def add(p, _):
        acc[places[p]] += received[p].astype(F32)
        return 0

    lax.fori_loop(0, received.shape[0], add, 0, unroll=4)


def first_sum(early, late):
    blocks, early_rows, width = early[0].shape
    late_rows = late[0].shape[1]
    shape = (blocks, early_rows + late_rows, width)

    def total(parts):
        value = parts[0][...].astype(F32)
        for part in parts[1:]:
            value = value + part[...].astype(F32)
        return value

    def kernel(*refs):
        *parts, result = refs
        result[:, :early_rows] = total(parts[:4])
        result[:, early_rows:] = total(parts[4:])

    return pl.pallas_call(
        kernel,
        out_shape=pltpu.HBM(shape, F32),
        grid=(1,),
        in_specs=[IN_VMEM] * 8,
        out_specs=whole(shape),
        compiler_params=pltpu.CompilerParams(vmem_limit_bytes=SMALL_VMEM),
        cost_estimate=cost(),
        name="first_sum",
    )(*early, *late)


def last_sum(places, received, so_far):
    blocks, _, width = so_far.shape
    rows = received.shape[1]

    def kernel(places, received, so_far, result, base, acc_a, acc_b, sems):
        later = pl.ds(EARLY_ROWS, rows)
        fetch = pltpu.make_async_copy(so_far.at[:, later], base, sems.at[0])
        fetch.start()
        acc_a[...] = jnp.zeros_like(acc_a)
        acc_b[...] = jnp.zeros_like(acc_b)

        def add(turn, _):
            for i, acc in enumerate((acc_a, acc_b)):
                p = turn * 2 + i
                acc[places[p]] += received[p].astype(F32)
            return 0

        lax.fori_loop(0, received.shape[0] // 2, add, 0, unroll=2)
        fetch.wait()
        base[...] += acc_a[:blocks] + acc_b[:blocks]
        store = pltpu.make_async_copy(base, result.at[:, later], sems.at[1])
        store.start()
        store.wait()

    return pl.pallas_call(
        kernel,
        out_shape=pltpu.HBM(so_far.shape, F32),
        grid_spec=pltpu.PrefetchScalarGridSpec(
            num_scalar_prefetch=1,
            grid=(1,),
            in_specs=[IN_VMEM, pl.BlockSpec(memory_space=pltpu.HBM)],
            out_specs=pl.BlockSpec(memory_space=pltpu.HBM),
            scratch_shapes=[
                pltpu.VMEM((blocks, rows, width), F32),
                pltpu.VMEM((blocks + 1, rows, width), F32),
                pltpu.VMEM((blocks + 1, rows, width), F32),
                pltpu.SemaphoreType.DMA((2,)),
            ],
        ),
        input_output_aliases={2: 0},
        compiler_params=pltpu.CompilerParams(vmem_limit_bytes=SMALL_VMEM),
        cost_estimate=cost(),
        name="last_sum",
    )(places, received, so_far)


def item_places(targets, block_count):
    destined = targets // block_count
    count = targets.shape[-1]
    earlier = jnp.arange(count)[:, None] > jnp.arange(count)[None, :]
    same = (destined[..., :, None] == destined[..., None, :]) & earlier
    return destined, jnp.sum(same.astype(jnp.int32), axis=-1)


def shards(wavefunction, left_env, right_env, block_left, block_right, channel_class, hop_target):
    block_count = wavefunction.shape[0]
    hop_count = hop_target.shape[1]
    owners = lax.axis_size("lsec") * lax.axis_size("rsec")
    item_count = block_count * hop_count
    capacity = 2 * ((item_count + owners - 1) // owners)
    slot_count = owners * capacity
    me = lax.axis_index("lsec") * lax.axis_size("rsec") + lax.axis_index("rsec")
    device = jnp.stack([lax.axis_index(axis) for axis in ("mpo", "lsec", "rsec")]).astype(jnp.int32)
    targets = hop_target.reshape(owners, item_count)
    own_targets = lax.dynamic_index_in_dim(targets, me, 0, False)
    own_early, early_slots, *parts = products(
        (block_left, block_right, channel_class, own_targets),
        owners,
        capacity,
        wavefunction,
        left_env,
        right_env,
        hop_count + 1,
    )

    own_late, parts = parts[:4], parts[4:]
    destined, slot = item_places(own_targets, block_count)
    position = destined * capacity + slot
    destined_all, slot_all = item_places(targets, block_count)
    mine = (destined_all == me)[:, :, None] & (
        slot_all[:, :, None] == jnp.arange(capacity, dtype=jnp.int32)
    )
    local = targets - (me + 1) * block_count
    places = jnp.sum(jnp.where(mine, local[:, :, None], 0), axis=1).reshape(slot_count)
    places = places + block_count

    beside = [(i, i ^ 1) for i in range(4)]
    mirror = [(i, 3 - i) for i in range(4)]
    across = [(i, (i + 2) % 4) for i in range(4)]

    def second(keep, got):
        return (keep[1].astype(F32) + got[1].astype(F32)).astype(BF16)

    early = lax.all_to_all(early_slots, ("lsec", "rsec"), 0, 0, tiled=True)
    keep_a, send_a, keep_b, send_b = parts
    got_a = lax.ppermute(send_a, "mpo", beside)
    got_b = lax.ppermute(send_b, "mpo", mirror)
    last_a = lax.ppermute(second(keep_a, got_a), "mpo", mirror)
    last_b = lax.ppermute(second(keep_b, got_b), "mpo", beside)
    slots = fill_slots(position, slot_count, (keep_a, got_a, last_a, keep_b, got_b, last_b))
    received = lax.all_to_all(slots, ("lsec", "rsec"), 0, 0, tiled=True)
    early, slots, *own_late = lax.optimization_barrier((early, slots, *own_late))

    def over_groups(parts):
        mine, *theirs = parts
        return [mine] + [
            lax.ppermute(part, "mpo", pairs)
            for part, pairs in zip(theirs, (beside, mirror, across))
        ]

    late = over_groups(own_late)
    early = over_groups(merge_early(device, places, early, own_early))
    return last_sum(places, received, first_sum(early, late))


def solution(mesh):
    in_specs = (
        P(("lsec", "rsec"), None, None),
        P("mpo", "lsec", None, None),
        P("mpo", "rsec", None, None),
        P(("lsec", "rsec")),
        P(("lsec", "rsec")),
        P(),
        P(),
    )
    out_specs = P(("lsec", "rsec"), "mpo", None)
    return jax.shard_map(shards, mesh=mesh, in_specs=in_specs, out_specs=out_specs, check_vma=False)
```
